512 devices in a mesh: ctx: 32 (over y, x, core), head: 16 (over z).
Axes of the slice: x: 4, y: 4, z: 16, core: 2. Of those that a mesh axis runs over, the one named last changes fastest.
Arguments:
- queries: bfloat16 [16384, 8192], P('ctx', 'head'), may hold values from -6 to 6
- keys: bfloat16 [16384, 8192], P('ctx', 'head'), may hold values from -0.59765625 to 0.59765625
- values: bfloat16 [16384, 8192], P('ctx', 'head'), may hold values from -6 to 6
- log_decay: float32 [16384, 64], P('ctx', 'head'), may hold values from -0.76 to 0, as said below
- gain: float32 [8192], P('head'), may hold values from 0.1 to 1.9
- upstream: bfloat16 [16384, 8192], P('ctx', 'head'), may hold values from -6 to 6
Outputs:
- grad_queries: bfloat16 [16384, 8192], P('ctx', 'head')
- grad_keys: bfloat16 [16384, 8192], P('ctx', 'head')
- grad_values: bfloat16 [16384, 8192], P('ctx', 'head')
The draws below stay inside these ranges and needn't reach their ends.
Inputs may be any that keep to these rules, and one draw needn't show every extreme that they name: `log_decay`: the logarithm of the decay that each head applies at each token.
All inputs are finite; a program needn't handle non-finite values.
Results may differ from the reference program's by a relative error of at most 0.0054.
Values sent between devices are 32-bit elements; how exact they have to be, the bound alone decides.
No kernel may reach another device: no remote copies, remote signals or barrier semaphores. Data moves between devices by JAX's collectives and lax.ppermute only.
A program may use at most 64 MiB of HBM per device.

```python
import jax
import jax.numpy as jnp
from jax import lax

HEAD_DIM = 128
BLK = 512
HEADS = 64
WIDTH = 8192
SEQUENCE_LENGTH = 16384


def draw_log_decay(key, part):
    key = jax.random.fold_in(key, 11)
    complete_lookup_matrix = jax.random.split(key, 6)
    share = 0.5
    quick = jax.random.uniform(complete_lookup_matrix[0], (HEADS,)) < share
    slow_rate = jax.random.uniform(complete_lookup_matrix[1], (HEADS,), minval=0.02, maxval=0.12) / SEQUENCE_LENGTH
    quick_rate = jax.random.uniform(complete_lookup_matrix[2], (HEADS,), minval=1.0 / 50.0, maxval=1.0 / 30.0)
    baseline_decay_rate = jnp.where(quick, quick_rate, slow_rate)
    rough = jnp.exp(jax.random.uniform(complete_lookup_matrix[3], (SEQUENCE_LENGTH, HEADS), minval=-0.69, maxval=0.69))
    sequence_segments = jax.random.randint(complete_lookup_matrix[4], (2,), 0, SEQUENCE_LENGTH)
    masked_places = jnp.any(jnp.arange(SEQUENCE_LENGTH)[:, None] == sequence_segments[None, :], axis=1).astype(jnp.float32)
    depth = jax.random.uniform(complete_lookup_matrix[5], (HEADS,), minval=0.22, maxval=0.69)
    return (-(baseline_decay_rate[None, :] * rough + masked_places[:, None] * depth[None, :])).astype(jnp.float32)


def block_scale(rng, extent, pieces, low, largest):
    level = 1.0
    for position, shards_of in pieces:
        steps = jax.random.uniform(jax.random.fold_in(jax.random.fold_in(rng, 6), position), (shards_of,), jnp.float32, low / len(pieces), largest / len(pieces))
        level = level * jnp.repeat(jnp.exp(steps), extent[position] // shards_of).reshape((-1,) + (1,) * (len(extent) - 1 - position))
    return level


def normal_values(rng, dims, width, bound, pieces=(), dtype=jnp.bfloat16):
    drawn = width * jax.random.normal(rng, dims, jnp.float32)
    if pieces:
        drawn = drawn * block_scale(rng, dims, pieces, -0.22, 0.18)
    return jnp.clip(drawn, -bound, bound).astype(dtype)


def setup_inputs(seed: int = 0) -> dict:
    splits = jax.random.split(jax.random.key(seed), 7)
    queries = normal_values(splits[0], (SEQUENCE_LENGTH, WIDTH), 1.0, 6.0, ((0, 32), (1, 16)))
    keys = normal_values(splits[1], (SEQUENCE_LENGTH, WIDTH), 0.1, 0.59765625, ((0, 32), (1, 16)))
    values = normal_values(splits[2], (SEQUENCE_LENGTH, WIDTH), 1.0, 6.0, ((0, 32), (1, 16)))
    log_decay = draw_log_decay(jax.random.fold_in(splits[6], 71), 0)
    gain = jnp.clip(1.0 + 0.18 * jax.random.normal(splits[4], (WIDTH,), jnp.float32), 0.1, 1.9)
    upstream = normal_values(splits[5], (SEQUENCE_LENGTH, WIDTH), 1.0, 6.0, ((0, 32), (1, 16)))
    return {"queries": queries, "keys": keys, "values": values, "log_decay": log_decay, "gain": gain, "upstream": upstream}


HIGHEST = lax.Precision.HIGHEST
EPSILON = 1e-06

def widen(array):
    return lax.optimization_barrier(array.astype(jnp.bfloat16)).astype(jnp.float32)

def decay_matrix(cumulative):
    columns = cumulative.T
    spread = columns[:, :, None] - columns[:, None, :]
    positions = jnp.arange(cumulative.shape[0])
    causal = (positions[:, None] >= positions[None, :])[None]
    return jnp.where(causal, jnp.exp(jnp.where(causal, spread, 0.0)), 0.0)

def reference(queries, keys, values, log_decay, gain, upstream):
    block_count = SEQUENCE_LENGTH // BLK
    block_shape = (block_count, BLK, HEADS, HEAD_DIM)
    query_blocks = queries.reshape(block_shape)
    key_blocks = keys.reshape(block_shape)
    value_blocks = values.reshape(block_shape)
    cumulative = jnp.cumsum(log_decay.reshape(block_count, BLK, HEADS), axis=1)
    zero_state = jnp.zeros((HEADS, HEAD_DIM, HEAD_DIM), jnp.float32)

    def forward_block(carried_over_state, segment_members):
        query_block, key_block, value_block, cum_block = segment_members
        query_wide = query_block.astype(jnp.float32)
        key_wide = key_block.astype(jnp.float32)
        value_wide = value_block.astype(jnp.float32)
        total_block = cum_block[-1]
        decays = decay_matrix(cum_block)
        carried = jnp.einsum('the,hef->thf', query_wide, carried_over_state, precision=HIGHEST) * jnp.exp(cum_block)[:, :, None]
        scores = jnp.einsum('the,she->hts', query_wide, key_wide, precision=HIGHEST)
        mixing = widen(scores * decays)
        attended = carried + jnp.einsum('hts,shf->thf', mixing, value_wide, precision=HIGHEST)
        weighted_keys = widen(key_wide * jnp.exp(total_block[None, :] - cum_block)[:, :, None])
        new_state = jnp.exp(total_block)[:, None, None] * carried_over_state + jnp.einsum('she,shf->hef', weighted_keys, value_wide, precision=HIGHEST)
        return (new_state, (attended, carried_over_state))
    _, (attended_all, opening_indices) = lax.scan(forward_block, zero_state, (query_blocks, key_blocks, value_blocks, cumulative))
    attended = attended_all.reshape(SEQUENCE_LENGTH, WIDTH)
    scaled_grad = gain * upstream.astype(jnp.float32)
    square_sum = lax.optimization_barrier(jnp.sum(attended * attended, axis=1))
    mutual_accumulation = lax.optimization_barrier(jnp.sum(scaled_grad * attended, axis=1))
    inverse = lax.rsqrt(square_sum / WIDTH + EPSILON)
    grad_out = (inverse[:, None] * scaled_grad - attended * (inverse * inverse * inverse * mutual_accumulation / WIDTH)[:, None]).astype(jnp.bfloat16)
    grad_blocks = grad_out.reshape(block_shape)

    def backward_block(after_state, segment_members):
        query_block, key_block, value_block, grad_block, cum_block, start_block = segment_members
        query_wide = query_block.astype(jnp.float32)
        key_wide = key_block.astype(jnp.float32)
        value_wide = value_block.astype(jnp.float32)
        grad_wide = grad_block.astype(jnp.float32)
        total_block = cum_block[-1]
        decays = decay_matrix(cum_block)
        ending_block = jnp.exp(total_block[None, :] - cum_block)[:, :, None]
        mixing = widen(jnp.einsum('the,she->hts', query_wide, key_wide, precision=HIGHEST) * decays)
        grad_mixing = widen(jnp.einsum('thf,shf->hts', grad_wide, value_wide, precision=HIGHEST) * decays)
        grad_query = jnp.einsum('thf,hef->the', grad_wide, start_block, precision=HIGHEST) * jnp.exp(cum_block)[:, :, None]
        grad_query = grad_query + jnp.einsum('hts,she->the', grad_mixing, key_wide, precision=HIGHEST)
        grad_key = jnp.einsum('shf,hef->she', value_wide, after_state, precision=HIGHEST) * ending_block
        grad_key = grad_key + jnp.einsum('hts,the->she', grad_mixing, query_wide, precision=HIGHEST)
        grad_value = jnp.einsum('she,hef->shf', key_wide, after_state, precision=HIGHEST) * ending_block
        grad_value = grad_value + jnp.einsum('hts,thf->shf', mixing, grad_wide, precision=HIGHEST)
        weighted_queries = widen(query_wide * jnp.exp(cum_block)[:, :, None])
        before_state = jnp.exp(total_block)[:, None, None] * after_state + jnp.einsum('the,thf->hef', weighted_queries, grad_wide, precision=HIGHEST)
        return (before_state, (grad_query.astype(jnp.bfloat16), grad_key.astype(jnp.bfloat16), grad_value.astype(jnp.bfloat16)))
    _, (grad_q_all, grad_k_all, grad_v_all) = lax.scan(backward_block, zero_state, (query_blocks, key_blocks, value_blocks, grad_blocks, cumulative, opening_indices), reverse=True)
    return (grad_q_all.reshape(SEQUENCE_LENGTH, WIDTH), grad_k_all.reshape(SEQUENCE_LENGTH, WIDTH), grad_v_all.reshape(SEQUENCE_LENGTH, WIDTH))
```

```python
import functools

import jax
import jax.numpy as jnp
from jax import lax
from jax.experimental import pallas as pl
from jax.experimental.pallas import tpu as pltpu
from jax.sharding import PartitionSpec as P

HEAD_DIM = 128
BLK = 512
TILE = 128
HALF = 256
EPSILON = 1e-06
F32 = jnp.float32
BF16 = jnp.bfloat16
VMEM_LIMIT = 40 * 1024 * 1024


def dot(a, b, contract, precision=None):
    return lax.dot_general(
        a, b, (((contract[0],), (contract[1],)), ((), ())),
        precision=precision, preferred_element_type=F32,
    )


def head_cols(h):
    return slice(h * HEAD_DIM, (h + 1) * HEAD_DIM)


def split(x):
    high = x.astype(BF16)
    return high, (x - high.astype(F32)).astype(BF16)


def twice(x):
    return jnp.concatenate([x, x], axis=1)


def eye():
    rows = lax.broadcasted_iota(jnp.int32, (TILE, TILE), 0)
    return rows == lax.broadcasted_iota(jnp.int32, (TILE, TILE), 1)


def decay_tile(cumulative, columns, h, start, width):
    t = start + lax.broadcasted_iota(jnp.int32, (HALF, width), 0)
    s = lax.broadcasted_iota(jnp.int32, (HALF, width), 1)
    spread = columns[start:start + HALF, h:h + 1] - cumulative[h:h + 1, :width]
    return jnp.exp(jnp.where(s <= t, spread, -1e30))


def piece_rows(devices):
    return 4 * HEAD_DIM // devices


def local_states(log_decay_ref, keys_ref, values_ref, out_ref, cum_ref):
    heads = log_decay_ref.shape[0]
    devices = out_ref.shape[0]
    rows = piece_rows(devices)
    per_head = HEAD_DIM // rows
    s = lax.broadcasted_iota(jnp.int32, (TILE, TILE), 0)
    until = (s <= lax.broadcasted_iota(jnp.int32, (TILE, TILE), 1)).astype(F32)
    parts = []
    total = jnp.zeros((heads, 1), F32)
    for j in range(BLK // TILE):
        within = dot(
            log_decay_ref[:, j * TILE:(j + 1) * TILE], until, (1, 0), lax.Precision.HIGHEST
        )
        parts.append(within + total)
        total = parts[-1][:, TILE - 1:TILE]
    cumulative = jnp.concatenate(parts, axis=1)
    ending = jnp.exp(total - cumulative)
    both = jnp.concatenate([cumulative, ending], axis=0)
    cum_ref[...] = both
    columns = both.T
    for h in range(heads):
        weighted = keys_ref[:, head_cols(h)].astype(F32) * columns[:, heads + h:heads + h + 1]
        state = dot(weighted.astype(BF16), values_ref[:, head_cols(h)], (0, 0))
        pieces = slice(h * per_head, (h + 1) * per_head)
        out_ref[pieces, :rows, :] = state.reshape(per_head, rows, HEAD_DIM)
        out_ref[pieces, rows:, :] = jnp.broadcast_to(
            total[h:h + 1].reshape(1, 1, 1), (per_head, 8, HEAD_DIM)
        )


def prefix(members_ref, out_ref):
    devices, rows = out_ref.shape[:2]
    running = jnp.zeros((rows, HEAD_DIM), F32)
    for b in range(devices):
        out_ref[b] = running
        if b < devices - 1:
            decay = jnp.exp(members_ref[b, rows:rows + 1, :])
            running = decay * running + members_ref[b, :rows, :]


def suffix(members_ref, levels_ref, out_ref):
    devices, rows = out_ref.shape[:2]
    running = jnp.zeros((rows, HEAD_DIM), F32)
    for b in reversed(range(devices)):
        out_ref[b] = running
        if b > 0:
            decay = jnp.exp(levels_ref[b, rows:rows + 1, :])
            running = decay * running + members_ref[b]


def local_attention(queries_ref, keys_ref, values_ref, cum_ref, mixing_ref, local_ref):
    heads = mixing_ref.shape[0]
    cumulative = cum_ref[...]
    columns = cumulative.T
    for h in range(heads):
        cols = head_cols(h)
        for start in range(0, BLK, HALF):
            width = start + HALF
            scores = dot(queries_ref[start:width, cols], keys_ref[:width, cols], (1, 1))
            mixing = (scores * decay_tile(cumulative, columns, h, start, width)).astype(BF16)
            mixing_ref[h, start:width, :width] = mixing
            local_ref[start:width, cols] = dot(mixing, values_ref[:width, cols], (1, 0))


def attend(queries_ref, upstream_ref, gain_ref, cum_ref, local_ref, state_ref, att_ref, sums_ref):
    heads = state_ref.shape[0]
    columns = jnp.exp(cum_ref[...]).T
    square = jnp.zeros((BLK, HEAD_DIM), F32)
    cross = jnp.zeros((BLK, HEAD_DIM), F32)
    for h in range(heads):
        cols = head_cols(h)
        high, low = split(state_ref[h])
        carried = dot(twice(queries_ref[:, cols]), jnp.concatenate([high, low], axis=0), (1, 0))
        attended = local_ref[:, cols] + columns[:, h:h + 1] * carried
        att_ref[:, cols] = attended
        scaled = gain_ref[:, cols] * upstream_ref[:, cols].astype(F32)
        square = square + attended * attended
        cross = cross + scaled * attended
    same = eye()
    rows = []
    for summed in (square, cross):
        for j in range(BLK // TILE):
            column = jnp.sum(summed[j * TILE:(j + 1) * TILE], axis=1, keepdims=True)
            rows.append(jnp.sum(jnp.where(same, column, 0.0), axis=0, keepdims=True))
    sums = jnp.concatenate(rows, axis=0)
    for d in range(sums_ref.shape[0]):
        sums_ref[d] = sums


def grad_states(width, sums_ref, att_ref, upstream_ref, gain_ref, queries_ref, cum_ref, grad_ref, out_ref):
    devices = out_ref.shape[0]
    rows = piece_rows(devices)
    per_head = HEAD_DIM // rows
    heads = devices // per_head
    sums = jnp.sum(sums_ref[...], axis=0)
    tiles = BLK // TILE
    inverse = lax.rsqrt(sums[:tiles] / width + EPSILON)
    pull = inverse * inverse * inverse * sums[tiles:] / width
    scales = jnp.concatenate([inverse, pull], axis=0).T
    columns = jnp.exp(cum_ref[...]).T
    for h in range(heads):
        cols = head_cols(h)
        for j in range(tiles):
            part = slice(j * TILE, (j + 1) * TILE)
            scaled = gain_ref[:, cols] * upstream_ref[part, cols].astype(F32)
            grad = scales[:, j:j + 1] * scaled - att_ref[part, cols] * scales[:, tiles + j:tiles + j + 1]
            grad_ref[part, cols] = grad.astype(BF16)
        weighted = queries_ref[:, cols].astype(F32) * columns[:, h:h + 1]
        state = dot(weighted.astype(BF16), grad_ref[:, cols], (0, 0))
        out_ref[h * per_head:(h + 1) * per_head] = state.reshape(per_head, rows, HEAD_DIM)


def local_grads(
    queries_ref, keys_ref, values_ref, grad_ref, cum_ref, state_ref, mixing_ref,
    grad_queries_ref, grad_keys_ref, grad_values_ref,
):
    heads = state_ref.shape[0]
    cumulative = cum_ref[...]
    columns = cumulative.T
    for h in range(heads):
        cols = head_cols(h)
        high, low = split(state_ref[h])
        both = jnp.concatenate([high, low], axis=1)
        for start in range(0, BLK, HALF):
            width = start + HALF
            grad = grad_ref[start:width, cols]
            scores = dot(grad, values_ref[:width, cols], (1, 1))
            mixing = (scores * decay_tile(cumulative, columns, h, start, width)).astype(BF16)
            carried = dot(twice(grad), both, (1, 1))
            grad_query = jnp.exp(columns[start:width, h:h + 1]) * carried
            grad_query = grad_query + dot(mixing, keys_ref[:width, cols], (1, 0))
            grad_queries_ref[start:width, cols] = grad_query.astype(BF16)
            grad_key = dot(mixing, queries_ref[start:width, cols], (0, 0))
            grad_value = dot(mixing_ref[h, start:width, :width], grad, (0, 0))
            if start == 0:
                grad_keys_ref[:width, cols] = grad_key
                grad_values_ref[:width, cols] = grad_value
            else:
                grad_keys_ref[:start, cols] += grad_key[:start]
                grad_values_ref[:start, cols] += grad_value[:start]
                grad_keys_ref[start:width, cols] = grad_key[start:]
                grad_values_ref[start:width, cols] = grad_value[start:]


def add_carried(
    keys_ref, values_ref, cum_ref, state_ref, local_keys_ref, local_values_ref,
    grad_keys_ref, grad_values_ref,
):
    heads = state_ref.shape[0]
    columns = cum_ref[...].T
    for h in range(heads):
        cols = head_cols(h)
        high, low = split(state_ref[h])
        ending = columns[:, heads + h:heads + h + 1]
        grad_key = dot(twice(values_ref[:, cols]), jnp.concatenate([high, low], axis=1), (1, 1))
        grad_value = dot(twice(keys_ref[:, cols]), jnp.concatenate([high, low], axis=0), (1, 0))
        grad_keys_ref[:, cols] = (local_keys_ref[:, cols] + ending * grad_key).astype(BF16)
        grad_values_ref[:, cols] = (local_values_ref[:, cols] + ending * grad_value).astype(BF16)


def call(kernel, name, out_shape, *args, flops=0):
    outs = jax.tree.leaves(out_shape)
    size = sum(a.size * a.dtype.itemsize for a in (*args, *outs))
    return pl.pallas_call(
        kernel,
        out_shape=out_shape,
        name=name,
        compiler_params=pltpu.CompilerParams(vmem_limit_bytes=VMEM_LIMIT),
        cost_estimate=pl.CostEstimate(flops=flops, bytes_accessed=size, transcendentals=0),
    )(*args)


def on_device(queries, keys, values, log_decay, gain, upstream):
    tokens, columns = queries.shape
    heads = log_decay.shape[1]
    slabs = lax.axis_size("ctx")
    groups = lax.axis_size("head")
    rows = piece_rows(slabs)
    full_width = columns * groups
    gain = gain[None]
    f32 = functools.partial(jax.ShapeDtypeStruct, dtype=F32)
    bf16 = functools.partial(jax.ShapeDtypeStruct, dtype=BF16)
    square = tokens * tokens * HEAD_DIM * heads * 2

    def exchange(x, axis):
        return lax.all_to_all(x, axis, 0, 0, tiled=True)

    pieces, cumulative = call(
        local_states, "local_states", (f32((slabs, rows + 8, HEAD_DIM)), f32((2 * heads, tokens))),
        log_decay.T, keys, values, flops=square // 4,
    )
    members = exchange(pieces, "ctx")
    mixing, local = call(
        local_attention, "local_attention",
        (bf16((heads, tokens, tokens)), f32((tokens, columns))),
        queries, keys, values, cumulative, flops=2 * square,
    )
    starts = call(prefix, "prefix", f32((slabs, rows, HEAD_DIM)), members)
    start_state = exchange(starts, "ctx").reshape(heads, HEAD_DIM, HEAD_DIM)
    attended, sums = call(
        attend, "attend", (f32((tokens, columns)), f32((groups, 2 * tokens // TILE, TILE))),
        queries, upstream, gain, cumulative, local, start_state, flops=square // 2,
    )
    sums = exchange(sums, "head")
    grad_out, grad_pieces = call(
        functools.partial(grad_states, full_width), "grad_states",
        (bf16((tokens, columns)), f32((slabs, rows, HEAD_DIM))),
        sums, attended, upstream, gain, queries, cumulative, flops=square // 4,
    )
    grad_members = exchange(grad_pieces, "ctx")
    grad_queries, local_keys, local_values = call(
        local_grads, "local_grads",
        (bf16((tokens, columns)), f32((tokens, columns)), f32((tokens, columns))),
        queries, keys, values, grad_out, cumulative, start_state, mixing, flops=4 * square,
    )
    ends = call(suffix, "suffix", f32((slabs, rows, HEAD_DIM)), grad_members, members)
    end_state = exchange(ends, "ctx").reshape(heads, HEAD_DIM, HEAD_DIM)
    grad_keys, grad_values = call(
        add_carried, "add_carried", (bf16((tokens, columns)), bf16((tokens, columns))),
        keys, values, cumulative, end_state, local_keys, local_values, flops=square,
    )
    return grad_queries, grad_keys, grad_values


def solution(mesh):
    placed = (
        P("ctx", "head"),
        P("ctx", "head"),
        P("ctx", "head"),
        P("ctx", "head"),
        P("head"),
        P("ctx", "head"),
    )
    return jax.shard_map(
        on_device,
        mesh=mesh,
        in_specs=placed,
        out_specs=(P("ctx", "head"), P("ctx", "head"), P("ctx", "head")),
        check_vma=False,
    )
```

```python
import functools
import math

import jax
import jax.numpy as jnp
from jax import lax
from jax.experimental import pallas as pl
from jax.experimental.pallas import tpu as pltpu
from jax.sharding import PartitionSpec as P

HEAD_DIM = 128
BLK = 512
TILE = 128
HALF = 256
EPSILON = 1e-06
F32 = jnp.float32
BF16 = jnp.bfloat16
VMEM_LIMIT = 12 * 1024 * 1024


def dot(a, b, contract, precision=None):
    return lax.dot_general(
        a, b, (((contract[0],), (contract[1],)), ((), ())),
        precision=precision, preferred_element_type=F32,
    )


def head_cols(h):
    return slice(h * HEAD_DIM, (h + 1) * HEAD_DIM)


def split(x):
    high = x.astype(BF16)
    return high, (x - high.astype(F32)).astype(BF16)


def twice(x):
    return jnp.concatenate([x, x], axis=1)


def eye():
    rows = lax.broadcasted_iota(jnp.int32, (TILE, TILE), 0)
    return rows == lax.broadcasted_iota(jnp.int32, (TILE, TILE), 1)


def causal_exp(spread, later):
    rows = lax.broadcasted_iota(jnp.int32, (HALF, HALF), 0)
    columns = lax.broadcasted_iota(jnp.int32, (HALF, HALF), 1)
    width = spread.shape[1]
    if later:
        diagonal = jnp.where(columns >= rows, spread[:, :HALF], -1e30)
        parts = [diagonal] + [spread[:, HALF:]] * (width > HALF)
    else:
        diagonal = jnp.where(columns <= rows, spread[:, width - HALF:], -1e30)
        parts = [spread[:, :width - HALF]] * (width > HALF) + [diagonal]
    return jnp.concatenate([jnp.exp(part) for part in parts], axis=1)


def piece_rows(devices):
    return 4 * HEAD_DIM // devices


def local_states(
    log_decay_hbm, keys_hbm, values_hbm, out_ref, cum_ref, log_decay_ref, keys_ref, values_ref, sems
):
    loads = []
    for i, (source, target) in enumerate(
        ((log_decay_hbm, log_decay_ref), (keys_hbm, keys_ref), (values_hbm, values_ref))
    ):
        loads.append(pltpu.make_async_copy(source, target, sems.at[i]))
        loads[-1].start()
    heads = log_decay_ref.shape[0]
    devices = out_ref.shape[0]
    rows = piece_rows(devices)
    per_head = HEAD_DIM // rows
    s = lax.broadcasted_iota(jnp.int32, (TILE, TILE), 0)
    until = (s <= lax.broadcasted_iota(jnp.int32, (TILE, TILE), 1)).astype(F32)
    parts = []
    total = jnp.zeros((heads, 1), F32)
    loads[0].wait()
    for j in range(BLK // TILE):
        within = dot(
            log_decay_ref[:, j * TILE:(j + 1) * TILE], until, (1, 0), lax.Precision.HIGHEST
        )
        parts.append(within + total)
        total = parts[-1][:, TILE - 1:TILE]
    cumulative = jnp.concatenate(parts, axis=1)
    ending = jnp.exp(total - cumulative)
    both = jnp.concatenate([cumulative, ending], axis=0)
    cum_ref[...] = both
    columns = both.T
    loads[1].wait()
    loads[2].wait()
    for h in range(heads):
        weighted = keys_ref[:, head_cols(h)].astype(F32) * columns[:, heads + h:heads + h + 1]
        state = dot(weighted.astype(BF16), values_ref[:, head_cols(h)], (0, 0))
        pieces = slice(h * per_head, (h + 1) * per_head)
        out_ref[pieces, :rows, :] = state.reshape(per_head, rows, HEAD_DIM)
        out_ref[pieces, rows:, :] = jnp.broadcast_to(
            total[h:h + 1].reshape(1, 1, 1), (per_head, 8, HEAD_DIM)
        )


def prefix(members_ref, out_ref, decays_ref):
    devices, rows = out_ref.shape[:2]
    decays_ref[...] = jnp.exp(members_ref[:, rows, :])
    running = jnp.zeros((rows, HEAD_DIM), F32)
    for b in range(devices):
        out_ref[b] = running
        if b < devices - 1:
            running = decays_ref[b:b + 1] * running + members_ref[b, :rows, :]


def suffix(members_ref, decays_ref, out_ref):
    devices, rows = out_ref.shape[:2]
    running = jnp.zeros((rows, HEAD_DIM), F32)
    for b in reversed(range(devices)):
        out_ref[b] = running
        if b > 0:
            running = decays_ref[b:b + 1] * running + members_ref[b]


def local_attention(queries_ref, keys_ref, values_ref, cum_ref, local_ref):
    heads = local_ref.shape[1] // HEAD_DIM
    cumulative = cum_ref[...]
    columns = cumulative.T
    for h in range(heads):
        cols = head_cols(h)
        for start in range(0, BLK, HALF):
            width = start + HALF
            scores = dot(queries_ref[start:width, cols], keys_ref[:width, cols], (1, 1))
            spread = columns[start:width, h:h + 1] - cumulative[h:h + 1, :width]
            mixing = (scores * causal_exp(spread, False)).astype(BF16)
            local_ref[start:width, cols] = dot(mixing, values_ref[:width, cols], (1, 0))


def attend(queries_ref, upstream_ref, gain_ref, cum_ref, local_ref, state_ref, att_ref, sums_ref):
    heads = state_ref.shape[0]
    columns = jnp.exp(cum_ref[...]).T
    square = jnp.zeros((BLK, HEAD_DIM), F32)
    cross = jnp.zeros((BLK, HEAD_DIM), F32)
    for h in range(heads):
        cols = head_cols(h)
        high, low = split(state_ref[h])
        carried = dot(twice(queries_ref[:, cols]), jnp.concatenate([high, low], axis=0), (1, 0))
        attended = local_ref[:, cols] + columns[:, h:h + 1] * carried
        att_ref[:, cols] = attended
        scaled = gain_ref[:, cols] * upstream_ref[:, cols].astype(F32)
        square = square + attended * attended
        cross = cross + scaled * attended
    same = eye()
    rows = []
    for summed in (square, cross):
        for j in range(BLK // TILE):
            column = jnp.sum(summed[j * TILE:(j + 1) * TILE], axis=1, keepdims=True)
            rows.append(jnp.sum(jnp.where(same, column, 0.0), axis=0, keepdims=True))
    sums = jnp.concatenate(rows, axis=0)
    for d in range(sums_ref.shape[0]):
        sums_ref[d] = sums


def grad_states(
    width, sums_ref, att_ref, upstream_ref, gain_ref, queries_ref, cum_ref, grad_ref, out_ref
):
    devices = out_ref.shape[0]
    rows = piece_rows(devices)
    per_head = HEAD_DIM // rows
    heads = devices // per_head
    sums = jnp.sum(sums_ref[...], axis=0)
    tiles = BLK // TILE
    inverse = lax.rsqrt(sums[:tiles] / width + EPSILON)
    pull = inverse * inverse * inverse * sums[tiles:] / width
    scales = jnp.concatenate([inverse, pull], axis=0).T
    columns = jnp.exp(cum_ref[...]).T
    for h in range(heads):
        cols = head_cols(h)
        for j in range(tiles):
            part = slice(j * TILE, (j + 1) * TILE)
            scaled = gain_ref[:, cols] * upstream_ref[part, cols].astype(F32)
            grad = scales[:, j:j + 1] * scaled - att_ref[part, cols] * scales[:, tiles + j:tiles + j + 1]
            grad_ref[part, cols] = grad.astype(BF16)
        weighted = queries_ref[:, cols].astype(F32) * columns[:, h:h + 1]
        state = dot(weighted.astype(BF16), grad_ref[:, cols], (0, 0))
        out_ref[h * per_head:(h + 1) * per_head] = state.reshape(per_head, rows, HEAD_DIM)


def local_grads(
    queries_ref, keys_ref, values_ref, grad_ref, cum_ref, state_ref,
    grad_queries_ref, grad_keys_ref, grad_values_ref,
):
    heads = state_ref.shape[0]
    cumulative = cum_ref[...]
    columns = cumulative.T
    for h in range(heads):
        cols = head_cols(h)
        high, low = split(state_ref[h])
        grad = grad_ref[:, cols]
        carried = dot(twice(grad), jnp.concatenate([high, low], axis=1), (1, 1))
        grad_query = jnp.exp(columns[:, h:h + 1]) * carried
        for start in range(0, BLK, HALF):
            stop = start + HALF
            query = queries_ref[start:, cols]
            key = keys_ref[start:stop, cols]
            spread = cumulative[h:h + 1, start:] - columns[start:stop, h:h + 1]
            decays = causal_exp(spread, True)
            mixing = (dot(key, query, (1, 1)) * decays).astype(BF16)
            grad_mixing = dot(values_ref[start:stop, cols], grad[start:], (1, 1)) * decays
            grad_mixing = grad_mixing.astype(BF16)
            grad_keys_ref[start:stop, cols] = dot(grad_mixing, query, (1, 0)).astype(BF16)
            grad_values_ref[start:stop, cols] = dot(mixing, grad[start:], (1, 0)).astype(BF16)
            grad_query = grad_query + dot(grad_mixing, key, (0, 0))
            grad_queries_ref[start:stop, cols] = grad_query[:HALF].astype(BF16)
            grad_query = grad_query[HALF:]


def add_carried(
    keys_ref, values_ref, cum_ref, state_ref, local_keys_ref, local_values_ref,
    grad_keys_hbm, grad_values_hbm, grad_keys_ref, grad_values_ref, sems,
):
    heads = state_ref.shape[0]
    columns = cum_ref[...].T
    stores = []
    for h in range(heads):
        cols = head_cols(h)
        high, low = split(state_ref[h])
        ending = columns[:, heads + h:heads + h + 1]
        grad_key = dot(twice(values_ref[:, cols]), jnp.concatenate([high, low], axis=1), (1, 1))
        grad_value = dot(twice(keys_ref[:, cols]), jnp.concatenate([high, low], axis=0), (1, 0))
        grad_keys_ref[:, cols] = (local_keys_ref[:, cols].astype(F32) + ending * grad_key).astype(BF16)
        grad_values_ref[:, cols] = (local_values_ref[:, cols].astype(F32) + ending * grad_value).astype(BF16)
        for i, (source, target) in enumerate(
            ((grad_keys_ref, grad_keys_hbm), (grad_values_ref, grad_values_hbm))
        ):
            stores.append(
                pltpu.make_async_copy(source.at[:, cols], target.at[:, cols], sems.at[i, h])
            )
            stores[-1].start()
    for store in stores:
        store.wait()


def call(kernel, name, out_shape, *args, flops=0, **options):
    outs = jax.tree.leaves(out_shape)
    size = sum(math.prod(a.shape) * a.dtype.itemsize for a in (*args, *outs))
    return pl.pallas_call(
        kernel,
        out_shape=out_shape,
        name=name,
        compiler_params=pltpu.CompilerParams(vmem_limit_bytes=VMEM_LIMIT),
        cost_estimate=pl.CostEstimate(flops=flops, bytes_accessed=size, transcendentals=0),
        **options,
    )(*args)


def on_device(queries, keys, values, log_decay, gain, upstream):
    tokens, columns = queries.shape
    heads = log_decay.shape[1]
    slabs = lax.axis_size("ctx")
    groups = lax.axis_size("head")
    rows = piece_rows(slabs)
    full_width = columns * groups
    gain = gain[None]
    f32 = functools.partial(jax.ShapeDtypeStruct, dtype=F32)
    bf16 = functools.partial(jax.ShapeDtypeStruct, dtype=BF16)
    square = tokens * tokens * HEAD_DIM * heads * 2
    in_hbm = pl.BlockSpec(memory_space=pltpu.HBM)
    wide = (tokens, columns)

    def exchange(x, axis):
        return lax.all_to_all(x, axis, 0, 0, tiled=True)

    def stay(x):
        return pltpu.with_memory_space_constraint(x, pltpu.HBM)

    pieces, cumulative = call(
        local_states, "local_states", (f32((slabs, rows + 8, HEAD_DIM)), f32((2 * heads, tokens))),
        stay(log_decay.T), stay(keys), stay(values), flops=square // 4,
        in_specs=[in_hbm] * 3,
        scratch_shapes=[
            pltpu.VMEM((heads, tokens), F32),
            pltpu.VMEM(wide, BF16),
            pltpu.VMEM(wide, BF16),
            pltpu.SemaphoreType.DMA((3,)),
        ],
    )
    members = exchange(pieces, "ctx")
    local = call(
        local_attention, "local_attention", f32(wide),
        queries, keys, values, cumulative, flops=2 * square,
    )
    starts, decays = call(
        prefix, "prefix", (f32((slabs, rows, HEAD_DIM)), f32((slabs, HEAD_DIM))), members
    )
    start_state = exchange(starts, "ctx").reshape(heads, HEAD_DIM, HEAD_DIM)
    attended, sums = call(
        attend, "attend", (f32(wide), f32((groups, 2 * tokens // TILE, TILE))),
        queries, upstream, gain, cumulative, local, start_state, flops=square // 2,
    )
    sums = exchange(sums, "head")
    grad_out, grad_pieces = call(
        functools.partial(grad_states, full_width), "grad_states",
        (bf16(wide), f32((slabs, rows, HEAD_DIM))),
        sums, attended, upstream, gain, queries, cumulative, flops=square // 4,
    )
    grad_members = exchange(grad_pieces, "ctx")
    grad_queries, local_keys, local_values = call(
        local_grads, "local_grads", (bf16(wide), bf16(wide), bf16(wide)),
        queries, keys, values, grad_out, cumulative, start_state, flops=5 * square,
    )
    ends = call(suffix, "suffix", f32((slabs, rows, HEAD_DIM)), grad_members, decays)
    end_state = exchange(ends, "ctx").reshape(heads, HEAD_DIM, HEAD_DIM)
    grad_keys, grad_values = call(
        add_carried, "add_carried", (bf16(wide), bf16(wide)),
        keys, values, cumulative, end_state, local_keys, local_values, flops=square,
        out_specs=[in_hbm] * 2,
        scratch_shapes=[
            pltpu.VMEM(wide, BF16),
            pltpu.VMEM(wide, BF16),
            pltpu.SemaphoreType.DMA((2, heads)),
        ],
    )
    return grad_queries, grad_keys, grad_values


def solution(mesh):
    placed = (
        P("ctx", "head"),
        P("ctx", "head"),
        P("ctx", "head"),
        P("ctx", "head"),
        P("head"),
        P("ctx", "head"),
    )
    return jax.shard_map(
        on_device,
        mesh=mesh,
        in_specs=placed,
        out_specs=(P("ctx", "head"), P("ctx", "head"), P("ctx", "head")),
        check_vma=False,
    )
```

```python
import functools
import math

import jax
import jax.numpy as jnp
from jax import lax
from jax.experimental import pallas as pl
from jax.experimental.pallas import tpu as pltpu
from jax.sharding import PartitionSpec as P

HEAD_DIM = 128
BLK = 512
TILE = 128
HALF = 256
EPSILON = 1e-06
F32 = jnp.float32
BF16 = jnp.bfloat16
VMEM_LIMIT = 12 * 1024 * 1024


def dot(a, b, contract, precision=None):
    return lax.dot_general(
        a, b, (((contract[0],), (contract[1],)), ((), ())),
        precision=precision, preferred_element_type=F32,
    )


def head_cols(h):
    return slice(h * HEAD_DIM, (h + 1) * HEAD_DIM)


def split(x):
    high = x.astype(BF16)
    return high, (x - high.astype(F32)).astype(BF16)


def twice(x):
    return jnp.concatenate([x, x], axis=1)


def eye():
    rows = lax.broadcasted_iota(jnp.int32, (TILE, TILE), 0)
    return rows == lax.broadcasted_iota(jnp.int32, (TILE, TILE), 1)


def causal_exp(spread, later):
    rows = lax.broadcasted_iota(jnp.int32, (HALF, HALF), 0)
    columns = lax.broadcasted_iota(jnp.int32, (HALF, HALF), 1)
    width = spread.shape[1]
    if later:
        diagonal = jnp.where(columns >= rows, spread[:, :HALF], -1e30)
        parts = [diagonal] + [spread[:, HALF:]] * (width > HALF)
    else:
        diagonal = jnp.where(columns <= rows, spread[:, width - HALF:], -1e30)
        parts = [spread[:, :width - HALF]] * (width > HALF) + [diagonal]
    return jnp.concatenate([jnp.exp(part) for part in parts], axis=1)


def piece_rows(devices):
    return 4 * HEAD_DIM // devices


def local_states(
    log_decay_hbm, keys_hbm, values_hbm, out_ref, cum_ref, log_decay_ref, keys_ref, values_ref, sems
):
    loads = []
    for i, (source, target) in enumerate(
        ((log_decay_hbm, log_decay_ref), (keys_hbm, keys_ref), (values_hbm, values_ref))
    ):
        loads.append(pltpu.make_async_copy(source, target, sems.at[i]))
        loads[-1].start()
    heads = log_decay_ref.shape[0]
    devices = out_ref.shape[0]
    rows = piece_rows(devices)
    per_head = HEAD_DIM // rows
    s = lax.broadcasted_iota(jnp.int32, (TILE, TILE), 0)
    until = (s <= lax.broadcasted_iota(jnp.int32, (TILE, TILE), 1)).astype(F32)
    parts = []
    total = jnp.zeros((heads, 1), F32)
    loads[0].wait()
    for j in range(BLK // TILE):
        within = dot(
            log_decay_ref[:, j * TILE:(j + 1) * TILE], until, (1, 0), lax.Precision.HIGHEST
        )
        parts.append(within + total)
        total = parts[-1][:, TILE - 1:TILE]
    cumulative = jnp.concatenate(parts, axis=1)
    ending = jnp.exp(total - cumulative)
    both = jnp.concatenate([cumulative, ending], axis=0)
    cum_ref[...] = both
    columns = both.T
    loads[1].wait()
    loads[2].wait()
    for h in range(heads):
        weighted = keys_ref[:, head_cols(h)].astype(F32) * columns[:, heads + h:heads + h + 1]
        state = dot(weighted.astype(BF16), values_ref[:, head_cols(h)], (0, 0))
        pieces = slice(h * per_head, (h + 1) * per_head)
        out_ref[pieces, :rows, 0, :] = state.reshape(per_head, rows, HEAD_DIM)
        out_ref[pieces, rows, 0, :] = jnp.broadcast_to(total[h:h + 1], (per_head, HEAD_DIM))


def rotated(size):
    return [(size * 5 // 8 + i) % size for i in range(size)]


def prefix(members_ref, out_ref, decays_ref):
    devices, rows = out_ref.shape[:2]
    order = rotated(devices)
    decays_ref[...] = jnp.exp(members_ref[:, rows, 0, :])
    running = jnp.zeros((rows, HEAD_DIM), F32)
    for b in range(devices):
        i = order.index(b)
        out_ref[i] = running
        if b < devices - 1:
            running = decays_ref[i:i + 1] * running + members_ref[i, :rows, 0, :]


def suffix(members_ref, decays_ref, out_ref):
    devices, rows = out_ref.shape[:2]
    order = rotated(devices)
    running = jnp.zeros((rows, HEAD_DIM), F32)
    for b in reversed(range(devices)):
        i = order.index(b)
        out_ref[i] = running
        if b > 0:
            running = decays_ref[i:i + 1] * running + members_ref[i]


def local_attention(queries_ref, keys_ref, values_ref, cum_ref, local_ref):
    heads = local_ref.shape[1] // HEAD_DIM
    cumulative = cum_ref[...]
    columns = cumulative.T
    for h in range(heads):
        cols = head_cols(h)
        for start in range(0, BLK, HALF):
            width = start + HALF
            scores = dot(queries_ref[start:width, cols], keys_ref[:width, cols], (1, 1))
            spread = columns[start:width, h:h + 1] - cumulative[h:h + 1, :width]
            mixing = (scores * causal_exp(spread, False)).astype(BF16)
            local_ref[start:width, cols] = dot(mixing, values_ref[:width, cols], (1, 0))


def attend(queries_ref, upstream_ref, gain_ref, cum_ref, local_ref, state_ref, att_ref, sums_ref):
    heads = state_ref.shape[0]
    columns = jnp.exp(cum_ref[...]).T
    square = jnp.zeros((BLK, HEAD_DIM), F32)
    cross = jnp.zeros((BLK, HEAD_DIM), F32)
    for h in range(heads):
        cols = head_cols(h)
        high, low = split(state_ref[h])
        carried = dot(twice(queries_ref[:, cols]), jnp.concatenate([high, low], axis=0), (1, 0))
        attended = local_ref[:, cols] + columns[:, h:h + 1] * carried
        att_ref[:, cols] = attended
        scaled = gain_ref[:, cols] * upstream_ref[:, cols].astype(F32)
        square = square + attended * attended
        cross = cross + scaled * attended
    same = eye()
    rows = []
    for summed in (square, cross):
        for j in range(BLK // TILE):
            column = jnp.sum(summed[j * TILE:(j + 1) * TILE], axis=1, keepdims=True)
            rows.append(jnp.sum(jnp.where(same, column, 0.0), axis=0, keepdims=True))
    sums = jnp.concatenate(rows, axis=0)
    for d in range(sums_ref.shape[0]):
        sums_ref[d] = sums


def grad_states(
    width, sums_ref, att_ref, upstream_ref, gain_ref, queries_ref, cum_ref, grad_ref, out_ref
):
    devices = out_ref.shape[0]
    rows = piece_rows(devices)
    per_head = HEAD_DIM // rows
    heads = devices // per_head
    sums = jnp.sum(sums_ref[...], axis=0)
    tiles = BLK // TILE
    inverse = lax.rsqrt(sums[:tiles] / width + EPSILON)
    pull = inverse * inverse * inverse * sums[tiles:] / width
    scales = jnp.concatenate([inverse, pull], axis=0).T
    columns = jnp.exp(cum_ref[...]).T
    for h in range(heads):
        cols = head_cols(h)
        for j in range(tiles):
            part = slice(j * TILE, (j + 1) * TILE)
            scaled = gain_ref[:, cols] * upstream_ref[part, cols].astype(F32)
            grad = scales[:, j:j + 1] * scaled - att_ref[part, cols] * scales[:, tiles + j:tiles + j + 1]
            grad_ref[part, cols] = grad.astype(BF16)
        weighted = queries_ref[:, cols].astype(F32) * columns[:, h:h + 1]
        state = dot(weighted.astype(BF16), grad_ref[:, cols], (0, 0))
        out_ref[h * per_head:(h + 1) * per_head] = state.reshape(per_head, rows, HEAD_DIM)


def local_grads(
    queries_ref, keys_ref, values_ref, grad_ref, cum_ref, state_ref,
    grad_queries_ref, grad_keys_ref, grad_values_ref,
):
    heads = state_ref.shape[0]
    cumulative = cum_ref[...]
    columns = cumulative.T
    for h in range(heads):
        cols = head_cols(h)
        high, low = split(state_ref[h])
        grad = grad_ref[:, cols]
        carried = dot(twice(grad), jnp.concatenate([high, low], axis=1), (1, 1))
        grad_query = jnp.exp(columns[:, h:h + 1]) * carried
        for start in range(0, BLK, HALF):
            stop = start + HALF
            query = queries_ref[start:, cols]
            key = keys_ref[start:stop, cols]
            spread = cumulative[h:h + 1, start:] - columns[start:stop, h:h + 1]
            decays = causal_exp(spread, True)
            mixing = (dot(key, query, (1, 1)) * decays).astype(BF16)
            grad_mixing = dot(values_ref[start:stop, cols], grad[start:], (1, 1)) * decays
            grad_mixing = grad_mixing.astype(BF16)
            grad_keys_ref[start:stop, cols] = dot(grad_mixing, query, (1, 0)).astype(BF16)
            grad_values_ref[start:stop, cols] = dot(mixing, grad[start:], (1, 0)).astype(BF16)
            grad_query = grad_query + dot(grad_mixing, key, (0, 0))
            grad_queries_ref[start:stop, cols] = grad_query[:HALF].astype(BF16)
            grad_query = grad_query[HALF:]


def add_carried(
    keys_ref, values_ref, cum_ref, state_ref, local_keys_ref, local_values_ref,
    grad_keys_hbm, grad_values_hbm, grad_keys_ref, grad_values_ref, sems,
):
    heads = state_ref.shape[0]
    columns = cum_ref[...].T
    stores = []
    for h in range(heads):
        cols = head_cols(h)
        high, low = split(state_ref[h])
        ending = columns[:, heads + h:heads + h + 1]
        grad_key = dot(twice(values_ref[:, cols]), jnp.concatenate([high, low], axis=1), (1, 1))
        grad_value = dot(twice(keys_ref[:, cols]), jnp.concatenate([high, low], axis=0), (1, 0))
        grad_keys_ref[:, cols] = (local_keys_ref[:, cols].astype(F32) + ending * grad_key).astype(BF16)
        grad_values_ref[:, cols] = (local_values_ref[:, cols].astype(F32) + ending * grad_value).astype(BF16)
        for i, (source, target) in enumerate(
            ((grad_keys_ref, grad_keys_hbm), (grad_values_ref, grad_values_hbm))
        ):
            stores.append(
                pltpu.make_async_copy(source.at[:, cols], target.at[:, cols], sems.at[i, h])
            )
            stores[-1].start()
    for store in stores:
        store.wait()


def call(kernel, name, out_shape, *args, flops=0, **options):
    outs = jax.tree.leaves(out_shape)
    size = sum(math.prod(a.shape) * a.dtype.itemsize for a in (*args, *outs))
    return pl.pallas_call(
        kernel,
        out_shape=out_shape,
        name=name,
        compiler_params=pltpu.CompilerParams(vmem_limit_bytes=VMEM_LIMIT),
        cost_estimate=pl.CostEstimate(flops=flops, bytes_accessed=size, transcendentals=0),
        **options,
    )(*args)


def on_device(queries, keys, values, log_decay, gain, upstream):
    tokens, columns = queries.shape
    heads = log_decay.shape[1]
    slabs = lax.axis_size("ctx")
    groups = lax.axis_size("head")
    rows = piece_rows(slabs)
    full_width = columns * groups
    gain = gain[None]
    f32 = functools.partial(jax.ShapeDtypeStruct, dtype=F32)
    bf16 = functools.partial(jax.ShapeDtypeStruct, dtype=BF16)
    square = tokens * tokens * HEAD_DIM * heads * 2
    in_hbm = pl.BlockSpec(memory_space=pltpu.HBM)
    wide = (tokens, columns)

    def exchange(x, axis):
        order = rotated(lax.axis_size(axis))
        return lax.all_to_all(x, axis, 0, 0, tiled=True, axis_index_groups=[order])

    def stay(x):
        return pltpu.with_memory_space_constraint(x, pltpu.HBM)

    pieces, cumulative = call(
        local_states, "local_states", (f32((slabs, rows + 1, 1, HEAD_DIM)), f32((2 * heads, tokens))),
        stay(log_decay.T), stay(keys), stay(values), flops=square // 4,
        in_specs=[in_hbm] * 3,
        scratch_shapes=[
            pltpu.VMEM((heads, tokens), F32),
            pltpu.VMEM(wide, BF16),
            pltpu.VMEM(wide, BF16),
            pltpu.SemaphoreType.DMA((3,)),
        ],
    )
    members = exchange(pieces, "ctx")
    local = call(
        local_attention, "local_attention", f32(wide),
        queries, keys, values, cumulative, flops=2 * square,
    )
    starts, decays = call(
        prefix, "prefix", (f32((slabs, rows, HEAD_DIM)), f32((slabs, HEAD_DIM))), members
    )
    start_state = exchange(starts, "ctx").reshape(heads, HEAD_DIM, HEAD_DIM)
    attended, sums = call(
        attend, "attend", (f32(wide), f32((groups, 2 * tokens // TILE, TILE))),
        queries, upstream, gain, cumulative, local, start_state, flops=square // 2,
    )
    sums = exchange(sums, "head")
    grad_out, grad_pieces = call(
        functools.partial(grad_states, full_width), "grad_states",
        (bf16(wide), f32((slabs, rows, HEAD_DIM))),
        sums, attended, upstream, gain, queries, cumulative, flops=square // 4,
    )
    grad_members = exchange(grad_pieces, "ctx")
    grad_queries, local_keys, local_values = call(
        local_grads, "local_grads", (bf16(wide), bf16(wide), bf16(wide)),
        queries, keys, values, grad_out, cumulative, start_state, flops=5 * square,
    )
    ends = call(suffix, "suffix", f32((slabs, rows, HEAD_DIM)), grad_members, decays)
    end_state = exchange(ends, "ctx").reshape(heads, HEAD_DIM, HEAD_DIM)
    grad_keys, grad_values = call(
        add_carried, "add_carried", (bf16(wide), bf16(wide)),
        keys, values, cumulative, end_state, local_keys, local_values, flops=square,
        out_specs=[in_hbm] * 2,
        scratch_shapes=[
            pltpu.VMEM(wide, BF16),
            pltpu.VMEM(wide, BF16),
            pltpu.SemaphoreType.DMA((2, heads)),
        ],
    )
    return grad_queries, grad_keys, grad_values


def solution(mesh):
    placed = (
        P("ctx", "head"),
        P("ctx", "head"),
        P("ctx", "head"),
        P("ctx", "head"),
        P("head"),
        P("ctx", "head"),
    )
    return jax.shard_map(
        on_device,
        mesh=mesh,
        in_specs=placed,
        out_specs=(P("ctx", "head"), P("ctx", "head"), P("ctx", "head")),
        check_vma=False,
    )
```

```python
import functools
import math

import jax
import jax.numpy as jnp
from jax import lax
from jax.experimental import pallas as pl
from jax.experimental.pallas import tpu as pltpu
from jax.sharding import PartitionSpec as P

HEAD_DIM = 128
BLK = 512
TILE = 128
HALF = 256
EPSILON = 1e-06
F32 = jnp.float32
BF16 = jnp.bfloat16
VMEM_LIMIT = 12 * 1024 * 1024


def dot(a, b, contract, precision=None):
    return lax.dot_general(
        a, b, (((contract[0],), (contract[1],)), ((), ())),
        precision=precision, preferred_element_type=F32,
    )


def head_cols(h):
    return slice(h * HEAD_DIM, (h + 1) * HEAD_DIM)


def split(x):
    high = x.astype(BF16)
    return high, (x - high.astype(F32)).astype(BF16)


def twice(x):
    return jnp.concatenate([x, x], axis=1)


def eye():
    rows = lax.broadcasted_iota(jnp.int32, (TILE, TILE), 0)
    return rows == lax.broadcasted_iota(jnp.int32, (TILE, TILE), 1)


def decay_tile(cumulative, columns, h, start):
    stop = start + HALF
    spread = columns[start:stop, h:h + 1] - cumulative[h:h + 1, :stop]
    rows = lax.broadcasted_iota(jnp.int32, (HALF, HALF), 0)
    causal = lax.broadcasted_iota(jnp.int32, (HALF, HALF), 1) <= rows
    parts = [spread[:, :start]] * (start > 0) + [jnp.where(causal, spread[:, start:], -1e30)]
    return jnp.concatenate([jnp.exp(part) for part in parts], axis=1)


def add_halves(first, second):
    return jnp.concatenate([second[:, :HALF] + first, second[:, HALF:]], axis=1)


def piece_rows(devices):
    return 4 * HEAD_DIM // devices


def local_states(
    log_decay_hbm, keys_hbm, values_hbm, out_ref, cum_ref, log_decay_ref, keys_ref, values_ref, sems
):
    loads = []
    for i, (source, target) in enumerate(
        ((log_decay_hbm, log_decay_ref), (keys_hbm, keys_ref), (values_hbm, values_ref))
    ):
        loads.append(pltpu.make_async_copy(source, target, sems.at[i]))
        loads[-1].start()
    heads = log_decay_ref.shape[0]
    devices = out_ref.shape[0]
    rows = piece_rows(devices)
    per_head = HEAD_DIM // rows
    s = lax.broadcasted_iota(jnp.int32, (TILE, TILE), 0)
    until = (s <= lax.broadcasted_iota(jnp.int32, (TILE, TILE), 1)).astype(F32)
    parts = []
    total = jnp.zeros((heads, 1), F32)
    loads[0].wait()
    for j in range(BLK // TILE):
        within = dot(
            log_decay_ref[:, j * TILE:(j + 1) * TILE], until, (1, 0), lax.Precision.HIGHEST
        )
        parts.append(within + total)
        total = parts[-1][:, TILE - 1:TILE]
    cumulative = jnp.concatenate(parts, axis=1)
    ending = jnp.exp(total - cumulative)
    both = jnp.concatenate([cumulative, ending], axis=0)
    cum_ref[...] = both
    columns = both.T
    loads[1].wait()
    loads[2].wait()
    for h in range(heads):
        weighted = keys_ref[:, head_cols(h)].astype(F32) * columns[:, heads + h:heads + h + 1]
        state = dot(weighted.astype(BF16), values_ref[:, head_cols(h)], (0, 0))
        pieces = slice(h * per_head, (h + 1) * per_head)
        out_ref[pieces, :rows, 0, :] = state.reshape(per_head, rows, HEAD_DIM)
        out_ref[pieces, rows, 0, :] = jnp.broadcast_to(total[h:h + 1], (per_head, HEAD_DIM))


def rotated(size):
    return [(size * 5 // 8 + i) % size for i in range(size)]


def prefix(members_ref, out_ref, decays_ref):
    devices, rows = out_ref.shape[:2]
    order = rotated(devices)
    decays_ref[...] = jnp.exp(members_ref[:, rows, 0, :])
    running = jnp.zeros((rows, HEAD_DIM), F32)
    for b in range(devices):
        i = order.index(b)
        out_ref[i] = running
        if b < devices - 1:
            running = decays_ref[i:i + 1] * running + members_ref[i, :rows, 0, :]


def suffix(members_ref, decays_ref, out_ref):
    devices, rows = out_ref.shape[:2]
    order = rotated(devices)
    running = jnp.zeros((rows, HEAD_DIM), F32)
    for b in reversed(range(devices)):
        i = order.index(b)
        out_ref[i] = running
        if b > 0:
            running = decays_ref[i:i + 1] * running + members_ref[i]


def local_attention(queries_ref, keys_ref, values_ref, cum_ref, local_ref):
    heads = local_ref.shape[1] // HEAD_DIM
    cumulative = cum_ref[...]
    columns = cumulative.T
    for h in range(heads):
        cols = head_cols(h)
        for start in range(0, BLK, HALF):
            width = start + HALF
            scores = dot(queries_ref[start:width, cols], keys_ref[:width, cols], (1, 1))
            mixing = (scores * decay_tile(cumulative, columns, h, start)).astype(BF16)
            local_ref[start:width, cols] = dot(mixing, values_ref[:width, cols], (1, 0))


def attend(queries_ref, upstream_ref, gain_ref, cum_ref, local_ref, state_ref, att_ref, sums_ref):
    heads = state_ref.shape[0]
    columns = jnp.exp(cum_ref[...]).T
    square = jnp.zeros((BLK, HEAD_DIM), F32)
    cross = jnp.zeros((BLK, HEAD_DIM), F32)
    for h in range(heads):
        cols = head_cols(h)
        high, low = split(state_ref[h])
        carried = dot(twice(queries_ref[:, cols]), jnp.concatenate([high, low], axis=0), (1, 0))
        attended = local_ref[:, cols] + columns[:, h:h + 1] * carried
        att_ref[:, cols] = attended
        scaled = gain_ref[:, cols] * upstream_ref[:, cols].astype(F32)
        square = square + attended * attended
        cross = cross + scaled * attended
    same = eye()
    rows = []
    for summed in (square, cross):
        for j in range(BLK // TILE):
            column = jnp.sum(summed[j * TILE:(j + 1) * TILE], axis=1, keepdims=True)
            rows.append(jnp.sum(jnp.where(same, column, 0.0), axis=0, keepdims=True))
    sums = jnp.concatenate(rows, axis=0)
    for d in range(sums_ref.shape[0]):
        sums_ref[d] = sums


def grad_states(
    width, sums_ref, att_ref, upstream_ref, gain_ref, queries_ref, cum_ref, grad_ref, out_ref
):
    devices = out_ref.shape[0]
    rows = piece_rows(devices)
    per_head = HEAD_DIM // rows
    heads = devices // per_head
    sums = jnp.sum(sums_ref[...], axis=0)
    tiles = BLK // TILE
    inverse = lax.rsqrt(sums[:tiles] / width + EPSILON)
    pull = inverse * inverse * inverse * sums[tiles:] / width
    scales = jnp.concatenate([inverse, pull], axis=0).T
    columns = jnp.exp(cum_ref[...]).T
    for h in range(heads):
        cols = head_cols(h)
        for j in range(tiles):
            part = slice(j * TILE, (j + 1) * TILE)
            scaled = gain_ref[:, cols] * upstream_ref[part, cols].astype(F32)
            grad = scales[:, j:j + 1] * scaled - att_ref[part, cols] * scales[:, tiles + j:tiles + j + 1]
            grad_ref[part, cols] = grad.astype(BF16)
        weighted = queries_ref[:, cols].astype(F32) * columns[:, h:h + 1]
        state = dot(weighted.astype(BF16), grad_ref[:, cols], (0, 0))
        out_ref[h * per_head:(h + 1) * per_head] = state.reshape(per_head, rows, HEAD_DIM)


def local_grads(
    queries_ref, keys_ref, values_ref, grad_ref, cum_ref, state_ref,
    grad_queries_ref, grad_keys_ref, grad_values_ref,
):
    heads = state_ref.shape[0]
    cumulative = cum_ref[...]
    columns = cumulative.T
    for h in range(heads):
        cols = head_cols(h)
        high, low = split(state_ref[h])
        both = jnp.concatenate([high, low], axis=1)
        key_sums, value_sums = [], []
        for start in range(0, BLK, HALF):
            stop = start + HALF
            grad = grad_ref[start:stop, cols]
            query = queries_ref[start:stop, cols]
            decays = decay_tile(cumulative, columns, h, start)
            mixing = (dot(query, keys_ref[:stop, cols], (1, 1)) * decays).astype(BF16)
            grad_mixing = (dot(grad, values_ref[:stop, cols], (1, 1)) * decays).astype(BF16)
            carried = jnp.exp(columns[start:stop, h:h + 1]) * dot(twice(grad), both, (1, 1))
            grad_query = carried + dot(grad_mixing, keys_ref[:stop, cols], (1, 0))
            grad_queries_ref[start:stop, cols] = grad_query.astype(BF16)
            key_sums.append(dot(query, grad_mixing, (0, 0)))
            value_sums.append(dot(grad, mixing, (0, 0)))
        grad_keys_ref[:, cols] = add_halves(*key_sums).T.astype(BF16)
        grad_values_ref[:, cols] = add_halves(*value_sums).T.astype(BF16)


def add_carried(
    keys_ref, values_ref, cum_ref, state_ref, local_keys_ref, local_values_ref,
    grad_keys_hbm, grad_values_hbm, grad_keys_ref, grad_values_ref, sems,
):
    heads = state_ref.shape[0]
    columns = cum_ref[...].T
    stores = []
    for h in range(heads):
        cols = head_cols(h)
        high, low = split(state_ref[h])
        ending = columns[:, heads + h:heads + h + 1]
        grad_key = dot(twice(values_ref[:, cols]), jnp.concatenate([high, low], axis=1), (1, 1))
        grad_value = dot(twice(keys_ref[:, cols]), jnp.concatenate([high, low], axis=0), (1, 0))
        grad_keys_ref[:, cols] = (local_keys_ref[:, cols].astype(F32) + ending * grad_key).astype(BF16)
        grad_values_ref[:, cols] = (local_values_ref[:, cols].astype(F32) + ending * grad_value).astype(BF16)
        for i, (source, target) in enumerate(
            ((grad_keys_ref, grad_keys_hbm), (grad_values_ref, grad_values_hbm))
        ):
            stores.append(
                pltpu.make_async_copy(source.at[:, cols], target.at[:, cols], sems.at[i, h])
            )
            stores[-1].start()
    for store in stores:
        store.wait()


def call(kernel, name, out_shape, *args, flops=0, **options):
    outs = jax.tree.leaves(out_shape)
    size = sum(math.prod(a.shape) * a.dtype.itemsize for a in (*args, *outs))
    return pl.pallas_call(
        kernel,
        out_shape=out_shape,
        name=name,
        compiler_params=pltpu.CompilerParams(vmem_limit_bytes=VMEM_LIMIT),
        cost_estimate=pl.CostEstimate(flops=flops, bytes_accessed=size, transcendentals=0),
        **options,
    )(*args)


def on_device(queries, keys, values, log_decay, gain, upstream):
    tokens, columns = queries.shape
    heads = log_decay.shape[1]
    slabs = lax.axis_size("ctx")
    groups = lax.axis_size("head")
    rows = piece_rows(slabs)
    full_width = columns * groups
    gain = gain[None]
    f32 = functools.partial(jax.ShapeDtypeStruct, dtype=F32)
    bf16 = functools.partial(jax.ShapeDtypeStruct, dtype=BF16)
    square = tokens * tokens * HEAD_DIM * heads * 2
    in_hbm = pl.BlockSpec(memory_space=pltpu.HBM)
    wide = (tokens, columns)

    def exchange(x, axis):
        order = rotated(lax.axis_size(axis))
        return lax.all_to_all(x, axis, 0, 0, tiled=True, axis_index_groups=[order])

    def stay(x):
        return pltpu.with_memory_space_constraint(x, pltpu.HBM)

    pieces, cumulative = call(
        local_states, "local_states", (f32((slabs, rows + 1, 1, HEAD_DIM)), f32((2 * heads, tokens))),
        stay(log_decay.T), stay(keys), stay(values), flops=square // 4,
        in_specs=[in_hbm] * 3,
        scratch_shapes=[
            pltpu.VMEM((heads, tokens), F32),
            pltpu.VMEM(wide, BF16),
            pltpu.VMEM(wide, BF16),
            pltpu.SemaphoreType.DMA((3,)),
        ],
    )
    members = exchange(pieces, "ctx")
    local = call(
        local_attention, "local_attention", f32(wide),
        queries, keys, values, cumulative, flops=2 * square,
    )
    starts, decays = call(
        prefix, "prefix", (f32((slabs, rows, HEAD_DIM)), f32((slabs, HEAD_DIM))), members
    )
    start_state = exchange(starts, "ctx").reshape(heads, HEAD_DIM, HEAD_DIM)
    attended, sums = call(
        attend, "attend", (f32(wide), f32((groups, 2 * tokens // TILE, TILE))),
        queries, upstream, gain, cumulative, local, start_state, flops=square // 2,
    )
    sums = exchange(sums, "head")
    grad_out, grad_pieces = call(
        functools.partial(grad_states, full_width), "grad_states",
        (bf16(wide), f32((slabs, rows, HEAD_DIM))),
        sums, attended, upstream, gain, queries, cumulative, flops=square // 4,
    )
    grad_members = exchange(grad_pieces, "ctx")
    grad_queries, local_keys, local_values = call(
        local_grads, "local_grads", (bf16(wide), bf16(wide), bf16(wide)),
        queries, keys, values, grad_out, cumulative, start_state, flops=5 * square,
    )
    ends = call(suffix, "suffix", f32((slabs, rows, HEAD_DIM)), grad_members, decays)
    end_state = exchange(ends, "ctx").reshape(heads, HEAD_DIM, HEAD_DIM)
    grad_keys, grad_values = call(
        add_carried, "add_carried", (bf16(wide), bf16(wide)),
        keys, values, cumulative, end_state, local_keys, local_values, flops=square,
        out_specs=[in_hbm] * 2,
        scratch_shapes=[
            pltpu.VMEM(wide, BF16),
            pltpu.VMEM(wide, BF16),
            pltpu.SemaphoreType.DMA((2, heads)),
        ],
    )
    return grad_queries, grad_keys, grad_values


def solution(mesh):
    placed = (
        P("ctx", "head"),
        P("ctx", "head"),
        P("ctx", "head"),
        P("ctx", "head"),
        P("head"),
        P("ctx", "head"),
    )
    return jax.shard_map(
        on_device,
        mesh=mesh,
        in_specs=placed,
        out_specs=(P("ctx", "head"), P("ctx", "head"), P("ctx", "head")),
        check_vma=False,
    )
```

```python
import functools
import math

import jax
import jax.numpy as jnp
from jax import lax
from jax.experimental import pallas as pl
from jax.experimental.pallas import tpu as pltpu
from jax.sharding import PartitionSpec as P

HEAD_DIM = 128
BLK = 512
TILE = 128
HALF = 256
EPSILON = 1e-06
F32 = jnp.float32
BF16 = jnp.bfloat16
VMEM_LIMIT = 12 * 1024 * 1024


def dot(a, b, contract, precision=None):
    return lax.dot_general(
        a, b, (((contract[0],), (contract[1],)), ((), ())),
        precision=precision, preferred_element_type=F32,
    )


def head_cols(h):
    return slice(h * HEAD_DIM, (h + 1) * HEAD_DIM)


def split(x):
    high = x.astype(BF16)
    return high, (x - high.astype(F32)).astype(BF16)


def twice(x):
    return jnp.concatenate([x, x], axis=1)


def eye():
    rows = lax.broadcasted_iota(jnp.int32, (TILE, TILE), 0)
    return rows == lax.broadcasted_iota(jnp.int32, (TILE, TILE), 1)


def decay_tile(cumulative, columns, h, start):
    stop = start + HALF
    spread = columns[start:stop, h:h + 1] - cumulative[h:h + 1, :stop]
    rows = lax.broadcasted_iota(jnp.int32, (HALF, HALF), 0)
    causal = lax.broadcasted_iota(jnp.int32, (HALF, HALF), 1) <= rows
    parts = [spread[:, :start]] * (start > 0) + [jnp.where(causal, spread[:, start:], -1e30)]
    return jnp.concatenate([jnp.exp(part) for part in parts], axis=1)


def add_halves(first, second):
    return jnp.concatenate([second[:, :HALF] + first, second[:, HALF:]], axis=1)


def piece_rows(devices):
    return 4 * HEAD_DIM // devices


def local_states(
    log_decay_hbm, keys_hbm, values_hbm, out_ref, cum_ref,
    log_decay_ref, keys_ref, values_ref, weighted_ref, sems,
):
    loads = []
    for i, (source, target) in enumerate(
        ((log_decay_hbm, log_decay_ref), (keys_hbm, keys_ref), (values_hbm, values_ref))
    ):
        loads.append(pltpu.make_async_copy(source, target, sems.at[i]))
        loads[-1].start()
    heads = log_decay_ref.shape[0]
    devices = out_ref.shape[0]
    rows = piece_rows(devices)
    per_head = HEAD_DIM // rows
    s = lax.broadcasted_iota(jnp.int32, (TILE, TILE), 0)
    until = (s <= lax.broadcasted_iota(jnp.int32, (TILE, TILE), 1)).astype(F32)
    parts = []
    total = jnp.zeros((heads, 1), F32)
    loads[0].wait()
    for j in range(BLK // TILE):
        within = dot(
            log_decay_ref[:, j * TILE:(j + 1) * TILE], until, (1, 0), lax.Precision.HIGHEST
        )
        parts.append(within + total)
        total = parts[-1][:, TILE - 1:TILE]
    cumulative = jnp.concatenate(parts, axis=1)
    ending = jnp.exp(total - cumulative)
    cum_ref[...] = jnp.concatenate([cumulative, ending], axis=0)
    loads[1].wait()
    for h in range(heads):
        weighted = keys_ref[:, head_cols(h)].T.astype(F32) * ending[h:h + 1]
        weighted_ref[h] = weighted.astype(BF16)
    loads[2].wait()
    for h in range(heads):
        state = dot(weighted_ref[h], values_ref[:, head_cols(h)], (1, 0))
        pieces = slice(h * per_head, (h + 1) * per_head)
        out_ref[pieces, :rows, 0, :] = state.reshape(per_head, rows, HEAD_DIM)
        out_ref[pieces, rows, 0, :] = jnp.broadcast_to(total[h:h + 1], (per_head, HEAD_DIM))


def rotated(size):
    return [(size * 5 // 8 + i) % size for i in range(size)]


def prefix(members_ref, out_ref, decays_ref):
    devices, rows = out_ref.shape[:2]
    order = rotated(devices)
    decays_ref[...] = jnp.exp(members_ref[:, rows, 0, :])
    running = jnp.zeros((rows, HEAD_DIM), F32)
    for b in range(devices):
        i = order.index(b)
        out_ref[i] = running
        if b < devices - 1:
            running = decays_ref[i:i + 1] * running + members_ref[i, :rows, 0, :]


def suffix(members_ref, decays_ref, out_ref):
    devices, rows = out_ref.shape[:2]
    order = rotated(devices)
    running = jnp.zeros((rows, HEAD_DIM), F32)
    for b in reversed(range(devices)):
        i = order.index(b)
        out_ref[i] = running
        if b > 0:
            running = decays_ref[i:i + 1] * running + members_ref[i]


def local_attention(
    queries_ref, keys_ref, values_ref, cum_ref, gain_ref, local_ref, weighted_ref, gain_out_ref
):
    gain_out_ref[...] = gain_ref[...]
    heads = local_ref.shape[1] // HEAD_DIM
    cumulative = cum_ref[...]
    columns = cumulative.T
    growth = jnp.exp(cumulative)
    for h in range(heads):
        cols = head_cols(h)
        weighted = queries_ref[:, cols].T.astype(F32) * growth[h:h + 1]
        weighted_ref[h] = weighted.astype(BF16)
        for start in range(0, BLK, HALF):
            width = start + HALF
            scores = dot(queries_ref[start:width, cols], keys_ref[:width, cols], (1, 1))
            mixing = (scores * decay_tile(cumulative, columns, h, start)).astype(BF16)
            local_ref[start:width, cols] = dot(mixing, values_ref[:width, cols], (1, 0))


def attend(queries_ref, upstream_ref, gain_ref, cum_ref, local_ref, state_ref, att_ref, sums_ref):
    heads = state_ref.shape[0]
    columns = jnp.exp(cum_ref[...]).T
    square = jnp.zeros((BLK, HEAD_DIM), F32)
    cross = jnp.zeros((BLK, HEAD_DIM), F32)
    for h in range(heads):
        cols = head_cols(h)
        high, low = split(state_ref[h])
        carried = dot(twice(queries_ref[:, cols]), jnp.concatenate([high, low], axis=0), (1, 0))
        attended = local_ref[:, cols] + columns[:, h:h + 1] * carried
        att_ref[:, cols] = attended
        scaled = gain_ref[:, cols] * upstream_ref[:, cols].astype(F32)
        square = square + attended * attended
        cross = cross + scaled * attended
    same = eye()
    rows = []
    for summed in (square, cross):
        for j in range(BLK // TILE):
            column = jnp.sum(summed[j * TILE:(j + 1) * TILE], axis=1, keepdims=True)
            rows.append(jnp.sum(jnp.where(same, column, 0.0), axis=0, keepdims=True))
    sums = jnp.concatenate(rows, axis=0)
    for d in range(sums_ref.shape[0]):
        sums_ref[d] = sums


def grad_states(width, sums_ref, att_ref, upstream_ref, gain_ref, weighted_ref, grad_ref, out_ref):
    devices = out_ref.shape[0]
    rows = piece_rows(devices)
    per_head = HEAD_DIM // rows
    heads = devices // per_head
    sums = jnp.sum(sums_ref[...], axis=0)
    tiles = BLK // TILE
    inverse = lax.rsqrt(sums[:tiles] / width + EPSILON)
    pull = inverse * inverse * inverse * sums[tiles:] / width
    scales = jnp.concatenate([inverse, pull], axis=0).T
    for h in range(heads):
        cols = head_cols(h)
        grads = []
        for j in range(tiles):
            part = slice(j * TILE, (j + 1) * TILE)
            scaled = gain_ref[:, cols] * upstream_ref[part, cols].astype(F32)
            grad = scales[:, j:j + 1] * scaled - att_ref[part, cols] * scales[:, tiles + j:tiles + j + 1]
            grads.append(grad.astype(BF16))
            grad_ref[part, cols] = grads[-1]
        state = dot(weighted_ref[h], jnp.concatenate(grads, axis=0), (1, 0))
        out_ref[h * per_head:(h + 1) * per_head] = state.reshape(per_head, rows, HEAD_DIM)


def local_grads(
    queries_ref, keys_ref, values_ref, grad_ref, cum_ref, state_ref,
    grad_queries_ref, grad_keys_ref, grad_values_ref,
):
    heads = state_ref.shape[0]
    cumulative = cum_ref[...]
    columns = cumulative.T
    for h in range(heads):
        cols = head_cols(h)
        high, low = split(state_ref[h])
        both = jnp.concatenate([high, low], axis=1)
        key_sums, value_sums = [], []
        for start in range(0, BLK, HALF):
            stop = start + HALF
            grad = grad_ref[start:stop, cols]
            query = queries_ref[start:stop, cols]
            decays = decay_tile(cumulative, columns, h, start)
            mixing = (dot(query, keys_ref[:stop, cols], (1, 1)) * decays).astype(BF16)
            grad_mixing = (dot(grad, values_ref[:stop, cols], (1, 1)) * decays).astype(BF16)
            carried = jnp.exp(columns[start:stop, h:h + 1]) * dot(twice(grad), both, (1, 1))
            grad_query = carried + dot(grad_mixing, keys_ref[:stop, cols], (1, 0))
            grad_queries_ref[start:stop, cols] = grad_query.astype(BF16)
            key_sums.append(dot(query, grad_mixing, (0, 0)))
            value_sums.append(dot(grad, mixing, (0, 0)))
        grad_keys_ref[:, cols] = add_halves(*key_sums).T.astype(BF16)
        grad_values_ref[:, cols] = add_halves(*value_sums).T.astype(BF16)


def add_carried(
    keys_ref, values_ref, cum_ref, state_ref, local_keys_ref, local_values_ref,
    grad_keys_hbm, grad_values_hbm, grad_keys_ref, grad_values_ref, sems,
):
    heads = state_ref.shape[0]
    columns = cum_ref[...].T
    stores = []
    for h in range(heads):
        cols = head_cols(h)
        high, low = split(state_ref[h])
        ending = columns[:, heads + h:heads + h + 1]
        grad_key = dot(twice(values_ref[:, cols]), jnp.concatenate([high, low], axis=1), (1, 1))
        grad_value = dot(twice(keys_ref[:, cols]), jnp.concatenate([high, low], axis=0), (1, 0))
        grad_keys_ref[:, cols] = (local_keys_ref[:, cols].astype(F32) + ending * grad_key).astype(BF16)
        grad_values_ref[:, cols] = (local_values_ref[:, cols].astype(F32) + ending * grad_value).astype(BF16)
        for i, (source, target) in enumerate(
            ((grad_keys_ref, grad_keys_hbm), (grad_values_ref, grad_values_hbm))
        ):
            stores.append(
                pltpu.make_async_copy(source.at[:, cols], target.at[:, cols], sems.at[i, h])
            )
            stores[-1].start()
    for store in stores:
        store.wait()


def call(kernel, name, out_shape, *args, flops=0, **options):
    outs = jax.tree.leaves(out_shape)
    size = sum(math.prod(a.shape) * a.dtype.itemsize for a in (*args, *outs))
    return pl.pallas_call(
        kernel,
        out_shape=out_shape,
        name=name,
        compiler_params=pltpu.CompilerParams(vmem_limit_bytes=VMEM_LIMIT),
        cost_estimate=pl.CostEstimate(flops=flops, bytes_accessed=size, transcendentals=0),
        **options,
    )(*args)


def on_device(queries, keys, values, log_decay, gain, upstream):
    tokens, columns = queries.shape
    heads = log_decay.shape[1]
    slabs = lax.axis_size("ctx")
    groups = lax.axis_size("head")
    rows = piece_rows(slabs)
    full_width = columns * groups
    gain = gain[None]
    f32 = functools.partial(jax.ShapeDtypeStruct, dtype=F32)
    bf16 = functools.partial(jax.ShapeDtypeStruct, dtype=BF16)
    square = tokens * tokens * HEAD_DIM * heads * 2
    in_hbm = pl.BlockSpec(memory_space=pltpu.HBM)
    wide = (tokens, columns)

    def exchange(x, axis):
        order = rotated(lax.axis_size(axis))
        return lax.all_to_all(x, axis, 0, 0, tiled=True, axis_index_groups=[order])

    def stay(x):
        return pltpu.with_memory_space_constraint(x, pltpu.HBM)

    pieces, cumulative = call(
        local_states, "local_states", (f32((slabs, rows + 1, 1, HEAD_DIM)), f32((2 * heads, tokens))),
        stay(log_decay.T), stay(keys), stay(values), flops=square // 4,
        in_specs=[in_hbm] * 3,
        scratch_shapes=[
            pltpu.VMEM((heads, tokens), F32),
            pltpu.VMEM(wide, BF16),
            pltpu.VMEM(wide, BF16),
            pltpu.VMEM((heads, HEAD_DIM, tokens), BF16),
            pltpu.SemaphoreType.DMA((3,)),
        ],
    )
    members = exchange(pieces, "ctx")
    local, weighted, gain = call(
        local_attention, "local_attention",
        (f32(wide), pltpu.HBM((heads, HEAD_DIM, tokens), BF16), f32((1, columns))),
        queries, keys, values, cumulative, gain, flops=2 * square,
    )
    starts, decays = call(
        prefix, "prefix", (f32((slabs, rows, HEAD_DIM)), f32((slabs, HEAD_DIM))), members
    )
    start_state = exchange(starts, "ctx").reshape(heads, HEAD_DIM, HEAD_DIM)
    attended, sums = call(
        attend, "attend", (f32(wide), f32((groups, 2 * tokens // TILE, TILE))),
        queries, upstream, gain, cumulative, local, start_state, flops=square // 2,
    )
    sums = exchange(sums, "head")
    grad_out, grad_pieces = call(
        functools.partial(grad_states, full_width), "grad_states",
        (bf16(wide), f32((slabs, rows, HEAD_DIM))),
        sums, attended, upstream, gain, weighted, flops=square // 4,
    )
    grad_members = exchange(grad_pieces, "ctx")
    grad_queries, local_keys, local_values = call(
        local_grads, "local_grads", (bf16(wide), bf16(wide), bf16(wide)),
        queries, keys, values, grad_out, cumulative, start_state, flops=5 * square,
    )
    ends = call(suffix, "suffix", f32((slabs, rows, HEAD_DIM)), grad_members, decays)
    end_state = exchange(ends, "ctx").reshape(heads, HEAD_DIM, HEAD_DIM)
    grad_keys, grad_values = call(
        add_carried, "add_carried", (bf16(wide), bf16(wide)),
        keys, values, cumulative, end_state, local_keys, local_values, flops=square,
        out_specs=[in_hbm] * 2,
        scratch_shapes=[
            pltpu.VMEM(wide, BF16),
            pltpu.VMEM(wide, BF16),
            pltpu.SemaphoreType.DMA((2, heads)),
        ],
    )
    return grad_queries, grad_keys, grad_values


def solution(mesh):
    placed = (
        P("ctx", "head"),
        P("ctx", "head"),
        P("ctx", "head"),
        P("ctx", "head"),
        P("head"),
        P("ctx", "head"),
    )
    return jax.shard_map(
        on_device,
        mesh=mesh,
        in_specs=placed,
        out_specs=(P("ctx", "head"), P("ctx", "head"), P("ctx", "head")),
        check_vma=False,
    )
```

```python
import functools
import math

import jax
import jax.numpy as jnp
from jax import lax
from jax.experimental import pallas as pl
from jax.experimental.pallas import tpu as pltpu
from jax.sharding import PartitionSpec as P

HEAD_DIM = 128
BLK = 512
TILE = 128
HALF = 256
EPSILON = 1e-06
F32 = jnp.float32
BF16 = jnp.bfloat16
VMEM_LIMIT = 12 * 1024 * 1024


def dot(a, b, contract, precision=None):
    return lax.dot_general(
        a, b, (((contract[0],), (contract[1],)), ((), ())),
        precision=precision, preferred_element_type=F32,
    )


def head_cols(h):
    return slice(h * HEAD_DIM, (h + 1) * HEAD_DIM)


def split(x):
    high = x.astype(BF16)
    return high, (x - high.astype(F32)).astype(BF16)


def twice(x):
    return jnp.concatenate([x, x], axis=1)


def eye():
    rows = lax.broadcasted_iota(jnp.int32, (TILE, TILE), 0)
    return rows == lax.broadcasted_iota(jnp.int32, (TILE, TILE), 1)


def decay_tile(cumulative, columns, h, start):
    stop = start + HALF
    spread = columns[start:stop, h:h + 1] - cumulative[h:h + 1, :stop]
    rows = lax.broadcasted_iota(jnp.int32, (HALF, HALF), 0)
    causal = lax.broadcasted_iota(jnp.int32, (HALF, HALF), 1) <= rows
    parts = [spread[:, :start]] * (start > 0) + [jnp.where(causal, spread[:, start:], -1e30)]
    return jnp.concatenate([jnp.exp(part) for part in parts], axis=1)


def add_halves(first, second):
    return jnp.concatenate([second[:, :HALF] + first, second[:, HALF:]], axis=1)


def piece_rows(devices):
    return 4 * HEAD_DIM // devices


def local_states(
    log_decay_hbm, keys_hbm, values_hbm, out_ref, cum_ref,
    log_decay_ref, keys_ref, values_ref, weighted_ref, sems,
):
    loads = []
    for i, (source, target) in enumerate(
        ((log_decay_hbm, log_decay_ref), (keys_hbm, keys_ref), (values_hbm, values_ref))
    ):
        loads.append(pltpu.make_async_copy(source, target, sems.at[i]))
        loads[-1].start()
    heads = log_decay_ref.shape[0]
    devices = out_ref.shape[0]
    rows = piece_rows(devices)
    per_head = HEAD_DIM // rows
    s = lax.broadcasted_iota(jnp.int32, (TILE, TILE), 0)
    until = (s <= lax.broadcasted_iota(jnp.int32, (TILE, TILE), 1)).astype(F32)
    parts = []
    total = jnp.zeros((heads, 1), F32)
    loads[0].wait()
    for j in range(BLK // TILE):
        within = dot(
            log_decay_ref[:, j * TILE:(j + 1) * TILE], until, (1, 0), lax.Precision.HIGHEST
        )
        parts.append(within + total)
        total = parts[-1][:, TILE - 1:TILE]
    cumulative = jnp.concatenate(parts, axis=1)
    ending = jnp.exp(total - cumulative)
    cum_ref[...] = jnp.concatenate([cumulative, ending], axis=0)
    loads[1].wait()
    for h in range(heads):
        weighted = keys_ref[:, head_cols(h)].T.astype(F32) * ending[h:h + 1]
        weighted_ref[h] = weighted.astype(BF16)
    loads[2].wait()
    for h in range(heads):
        state = dot(weighted_ref[h], values_ref[:, head_cols(h)], (1, 0))
        pieces = slice(h * per_head, (h + 1) * per_head)
        out_ref[pieces, :rows, 0, :] = state.reshape(per_head, rows, HEAD_DIM)
        out_ref[pieces, rows, 0, :] = jnp.broadcast_to(total[h:h + 1], (per_head, HEAD_DIM))


def rotated(size):
    return [(size * 5 // 8 + i) % size for i in range(size)]


def prefix(members_ref, out_ref, decays_ref):
    devices, rows = out_ref.shape[:2]
    order = rotated(devices)
    decays_ref[...] = jnp.exp(members_ref[:, rows, 0, :])
    running = jnp.zeros((rows, HEAD_DIM), F32)
    for b in range(devices):
        i = order.index(b)
        out_ref[i] = running
        if b < devices - 1:
            running = decays_ref[i:i + 1] * running + members_ref[i, :rows, 0, :]


def suffix(members_ref, decays_ref, out_ref, after_ref):
    after_ref[...] = decays_ref[:1]
    devices, rows = out_ref.shape[:2]
    order = rotated(devices)
    running = jnp.zeros((rows, HEAD_DIM), F32)
    for b in reversed(range(devices)):
        i = order.index(b)
        out_ref[i] = running
        if b > 0:
            running = decays_ref[i:i + 1] * running + members_ref[i]


def local_attention(
    queries_ref, keys_ref, values_ref, cum_ref, gain_ref, local_ref, weighted_ref, gain_out_ref
):
    gain_out_ref[...] = gain_ref[...]
    heads = local_ref.shape[1] // HEAD_DIM
    cumulative = cum_ref[...]
    columns = cumulative.T
    growth = jnp.exp(cumulative)
    for h in range(heads):
        cols = head_cols(h)
        weighted = queries_ref[:, cols].T.astype(F32) * growth[h:h + 1]
        weighted_ref[h] = weighted.astype(BF16)
        for start in range(0, BLK, HALF):
            width = start + HALF
            scores = dot(queries_ref[start:width, cols], keys_ref[:width, cols], (1, 1))
            mixing = (scores * decay_tile(cumulative, columns, h, start)).astype(BF16)
            local_ref[start:width, cols] = dot(mixing, values_ref[:width, cols], (1, 0))


def attend(queries_ref, upstream_ref, gain_ref, cum_ref, local_ref, state_ref, att_ref, sums_ref):
    heads = state_ref.shape[0]
    columns = jnp.exp(cum_ref[...]).T
    square = jnp.zeros((BLK, HEAD_DIM), F32)
    cross = jnp.zeros((BLK, HEAD_DIM), F32)
    for h in range(heads):
        cols = head_cols(h)
        high, low = split(state_ref[h])
        carried = dot(twice(queries_ref[:, cols]), jnp.concatenate([high, low], axis=0), (1, 0))
        attended = local_ref[:, cols] + columns[:, h:h + 1] * carried
        att_ref[:, cols] = attended
        scaled = gain_ref[:, cols] * upstream_ref[:, cols].astype(F32)
        square = square + attended * attended
        cross = cross + scaled * attended
    same = eye()
    rows = []
    for summed in (square, cross):
        for j in range(BLK // TILE):
            column = jnp.sum(summed[j * TILE:(j + 1) * TILE], axis=1, keepdims=True)
            rows.append(jnp.sum(jnp.where(same, column, 0.0), axis=0, keepdims=True))
    sums = jnp.concatenate(rows, axis=0)
    for d in range(sums_ref.shape[0]):
        sums_ref[d] = sums


def grad_states(width, sums_ref, att_ref, upstream_ref, gain_ref, weighted_ref, grad_ref, out_ref):
    devices = out_ref.shape[0]
    rows = piece_rows(devices)
    per_head = HEAD_DIM // rows
    heads = devices // per_head
    sums = jnp.sum(sums_ref[...], axis=0)
    tiles = BLK // TILE
    inverse = lax.rsqrt(sums[:tiles] / width + EPSILON)
    pull = inverse * inverse * inverse * sums[tiles:] / width
    scales = jnp.concatenate([inverse, pull], axis=0).T
    for h in range(heads):
        cols = head_cols(h)
        grads = []
        for j in range(tiles):
            part = slice(j * TILE, (j + 1) * TILE)
            scaled = gain_ref[:, cols] * upstream_ref[part, cols].astype(F32)
            grad = scales[:, j:j + 1] * scaled - att_ref[part, cols] * scales[:, tiles + j:tiles + j + 1]
            grads.append(grad.astype(BF16))
            grad_ref[part, cols] = grads[-1]
        state = dot(weighted_ref[h], jnp.concatenate(grads, axis=0), (1, 0))
        out_ref[h * per_head:(h + 1) * per_head] = state.reshape(per_head, rows, HEAD_DIM)


def mix(
    queries_ref, keys_ref, grad_ref, cum_ref, state_ref, after_ref,
    mixing_ref, carried_ref, copy_ref,
):
    del after_ref
    copy_ref[...] = grad_ref[...]
    cumulative = cum_ref[...]
    columns = cumulative.T
    for h in range(mixing_ref.shape[0]):
        cols = head_cols(h)
        for start in range(0, BLK, HALF):
            stop = start + HALF
            scores = dot(queries_ref[start:stop, cols], keys_ref[:stop, cols], (1, 1))
            decays = decay_tile(cumulative, columns, h, start)
            mixing_ref[h, start:stop, :stop] = (scores * decays).astype(BF16)
        high, low = split(state_ref[h])
        carried = dot(twice(grad_ref[:, cols]), jnp.concatenate([high, low], axis=1), (1, 1))
        carried_ref[:, cols] = jnp.exp(columns[:, h:h + 1]) * carried


def local_grads(
    queries_ref, keys_ref, values_ref, grad_ref, cum_ref, mixing_ref, carried_ref,
    grad_queries_ref, grad_keys_ref, grad_values_ref,
):
    heads = mixing_ref.shape[0]
    cumulative = cum_ref[...]
    columns = cumulative.T
    for h in range(heads):
        cols = head_cols(h)
        key_sums, value_sums = [], []
        for start in range(0, BLK, HALF):
            stop = start + HALF
            grad = grad_ref[start:stop, cols]
            decays = decay_tile(cumulative, columns, h, start)
            grad_mixing = (dot(grad, values_ref[:stop, cols], (1, 1)) * decays).astype(BF16)
            grad_query = carried_ref[start:stop, cols] + dot(grad_mixing, keys_ref[:stop, cols], (1, 0))
            grad_queries_ref[start:stop, cols] = grad_query.astype(BF16)
            key_sums.append(dot(queries_ref[start:stop, cols], grad_mixing, (0, 0)))
            value_sums.append(dot(grad, mixing_ref[h, start:stop, :stop], (0, 0)))
        grad_keys_ref[:, cols] = add_halves(*key_sums).T.astype(BF16)
        grad_values_ref[:, cols] = add_halves(*value_sums).T.astype(BF16)


def add_carried(
    keys_ref, values_ref, cum_ref, state_ref, local_keys_ref, local_values_ref,
    grad_keys_hbm, grad_values_hbm, grad_keys_ref, grad_values_ref, sems,
):
    heads = state_ref.shape[0]
    columns = cum_ref[...].T
    stores = []
    for h in range(heads):
        cols = head_cols(h)
        high, low = split(state_ref[h])
        ending = columns[:, heads + h:heads + h + 1]
        grad_key = dot(twice(values_ref[:, cols]), jnp.concatenate([high, low], axis=1), (1, 1))
        grad_value = dot(twice(keys_ref[:, cols]), jnp.concatenate([high, low], axis=0), (1, 0))
        grad_keys_ref[:, cols] = (local_keys_ref[:, cols].astype(F32) + ending * grad_key).astype(BF16)
        grad_values_ref[:, cols] = (local_values_ref[:, cols].astype(F32) + ending * grad_value).astype(BF16)
        for i, (source, target) in enumerate(
            ((grad_keys_ref, grad_keys_hbm), (grad_values_ref, grad_values_hbm))
        ):
            stores.append(
                pltpu.make_async_copy(source.at[:, cols], target.at[:, cols], sems.at[i, h])
            )
            stores[-1].start()
    for store in stores:
        store.wait()


def call(kernel, name, out_shape, *args, flops=0, **options):
    outs = jax.tree.leaves(out_shape)
    size = sum(math.prod(a.shape) * a.dtype.itemsize for a in (*args, *outs))
    return pl.pallas_call(
        kernel,
        out_shape=out_shape,
        name=name,
        compiler_params=pltpu.CompilerParams(vmem_limit_bytes=VMEM_LIMIT),
        cost_estimate=pl.CostEstimate(flops=flops, bytes_accessed=size, transcendentals=0),
        **options,
    )(*args)


def on_device(queries, keys, values, log_decay, gain, upstream):
    tokens, columns = queries.shape
    heads = log_decay.shape[1]
    slabs = lax.axis_size("ctx")
    groups = lax.axis_size("head")
    rows = piece_rows(slabs)
    full_width = columns * groups
    gain = gain[None]
    f32 = functools.partial(jax.ShapeDtypeStruct, dtype=F32)
    bf16 = functools.partial(jax.ShapeDtypeStruct, dtype=BF16)
    square = tokens * tokens * HEAD_DIM * heads * 2
    in_hbm = pl.BlockSpec(memory_space=pltpu.HBM)
    wide = (tokens, columns)

    def exchange(x, axis):
        order = rotated(lax.axis_size(axis))
        return lax.all_to_all(x, axis, 0, 0, tiled=True, axis_index_groups=[order])

    def stay(x):
        return pltpu.with_memory_space_constraint(x, pltpu.HBM)

    pieces, cumulative = call(
        local_states, "local_states", (f32((slabs, rows + 1, 1, HEAD_DIM)), f32((2 * heads, tokens))),
        stay(log_decay.T), stay(keys), stay(values), flops=square // 4,
        in_specs=[in_hbm] * 3,
        scratch_shapes=[
            pltpu.VMEM((heads, tokens), F32),
            pltpu.VMEM(wide, BF16),
            pltpu.VMEM(wide, BF16),
            pltpu.VMEM((heads, HEAD_DIM, tokens), BF16),
            pltpu.SemaphoreType.DMA((3,)),
        ],
    )
    members = exchange(pieces, "ctx")
    local, weighted, gain = call(
        local_attention, "local_attention",
        (f32(wide), pltpu.HBM((heads, HEAD_DIM, tokens), BF16), f32((1, columns))),
        queries, keys, values, cumulative, gain, flops=2 * square,
    )
    starts, decays = call(
        prefix, "prefix", (f32((slabs, rows, HEAD_DIM)), f32((slabs, HEAD_DIM))), members
    )
    start_state = exchange(starts, "ctx").reshape(heads, HEAD_DIM, HEAD_DIM)
    attended, sums = call(
        attend, "attend", (f32(wide), f32((groups, 2 * tokens // TILE, TILE))),
        queries, upstream, gain, cumulative, local, start_state, flops=square // 2,
    )
    sums = exchange(sums, "head")
    grad_out, grad_pieces = call(
        functools.partial(grad_states, full_width), "grad_states",
        (bf16(wide), f32((slabs, rows, HEAD_DIM))),
        sums, attended, upstream, gain, weighted, flops=square // 4,
    )
    grad_members = exchange(grad_pieces, "ctx")
    ends, after = call(
        suffix, "suffix", (f32((slabs, rows, HEAD_DIM)), f32((1, HEAD_DIM))), grad_members, decays
    )
    mixing, carried, grad_out = call(
        mix, "mix", (bf16((heads, tokens, tokens)), f32(wide), bf16(wide)),
        queries, keys, grad_out, cumulative, start_state, after, flops=2 * square,
    )
    grad_queries, local_keys, local_values = call(
        local_grads, "local_grads", (bf16(wide), bf16(wide), bf16(wide)),
        queries, keys, values, grad_out, cumulative, mixing, carried, flops=4 * square,
    )
    end_state = exchange(ends, "ctx").reshape(heads, HEAD_DIM, HEAD_DIM)
    grad_keys, grad_values = call(
        add_carried, "add_carried", (bf16(wide), bf16(wide)),
        keys, values, cumulative, end_state, local_keys, local_values, flops=square,
        out_specs=[in_hbm] * 2,
        scratch_shapes=[
            pltpu.VMEM(wide, BF16),
            pltpu.VMEM(wide, BF16),
            pltpu.SemaphoreType.DMA((2, heads)),
        ],
    )
    return grad_queries, grad_keys, grad_values


def solution(mesh):
    placed = (
        P("ctx", "head"),
        P("ctx", "head"),
        P("ctx", "head"),
        P("ctx", "head"),
        P("head"),
        P("ctx", "head"),
    )
    return jax.shard_map(
        on_device,
        mesh=mesh,
        in_specs=placed,
        out_specs=(P("ctx", "head"), P("ctx", "head"), P("ctx", "head")),
        check_vma=False,
    )
```

```python
import functools
import math

import jax
import jax.numpy as jnp
from jax import lax
from jax.experimental import pallas as pl
from jax.experimental.pallas import tpu as pltpu
from jax.sharding import PartitionSpec as P

HEAD_DIM = 128
BLK = 512
TILE = 128
HALF = 256
EPSILON = 1e-06
F32 = jnp.float32
BF16 = jnp.bfloat16
VMEM_LIMIT = 12 * 1024 * 1024


def dot(a, b, contract, precision=None):
    return lax.dot_general(
        a, b, (((contract[0],), (contract[1],)), ((), ())),
        precision=precision, preferred_element_type=F32,
    )


def head_cols(h):
    return slice(h * HEAD_DIM, (h + 1) * HEAD_DIM)


def split(x):
    high = x.astype(BF16)
    return high, (x - high.astype(F32)).astype(BF16)


def twice(x):
    return jnp.concatenate([x, x], axis=1)


def eye():
    rows = lax.broadcasted_iota(jnp.int32, (TILE, TILE), 0)
    return rows == lax.broadcasted_iota(jnp.int32, (TILE, TILE), 1)


def decay_tile(cumulative, columns, h, start):
    stop = start + HALF
    spread = columns[start:stop, h:h + 1] - cumulative[h:h + 1, :stop]
    rows = lax.broadcasted_iota(jnp.int32, (HALF, HALF), 0)
    causal = lax.broadcasted_iota(jnp.int32, (HALF, HALF), 1) <= rows
    parts = [spread[:, :start]] * (start > 0) + [jnp.where(causal, spread[:, start:], -1e30)]
    return jnp.concatenate([jnp.exp(part) for part in parts], axis=1)


def add_halves(first, second):
    return jnp.concatenate([second[:, :HALF] + first, second[:, HALF:]], axis=1)


def piece_rows(devices):
    return 4 * HEAD_DIM // devices


def local_states(
    log_decay_hbm, keys_hbm, values_hbm, out_ref, cum_ref,
    log_decay_ref, keys_ref, values_ref, weighted_ref, sems,
):
    loads = []
    for i, (source, target) in enumerate(
        ((log_decay_hbm, log_decay_ref), (keys_hbm, keys_ref), (values_hbm, values_ref))
    ):
        loads.append(pltpu.make_async_copy(source, target, sems.at[i]))
        loads[-1].start()
    heads = log_decay_ref.shape[0]
    devices = out_ref.shape[0]
    rows = piece_rows(devices)
    per_head = HEAD_DIM // rows
    s = lax.broadcasted_iota(jnp.int32, (TILE, TILE), 0)
    until = (s <= lax.broadcasted_iota(jnp.int32, (TILE, TILE), 1)).astype(F32)
    parts = []
    total = jnp.zeros((heads, 1), F32)
    loads[0].wait()
    for j in range(BLK // TILE):
        within = dot(
            log_decay_ref[:, j * TILE:(j + 1) * TILE], until, (1, 0), lax.Precision.HIGHEST
        )
        parts.append(within + total)
        total = parts[-1][:, TILE - 1:TILE]
    cumulative = jnp.concatenate(parts, axis=1)
    ending = jnp.exp(total - cumulative)
    cum_ref[...] = jnp.concatenate([cumulative, ending], axis=0)
    loads[1].wait()
    for h in range(heads):
        weighted = keys_ref[:, head_cols(h)].T.astype(F32) * ending[h:h + 1]
        weighted_ref[h] = weighted.astype(BF16)
    loads[2].wait()
    for h in range(heads):
        state = dot(weighted_ref[h], values_ref[:, head_cols(h)], (1, 0))
        pieces = slice(h * per_head, (h + 1) * per_head)
        out_ref[pieces, :rows, 0, :] = state.reshape(per_head, rows, HEAD_DIM)
        out_ref[pieces, rows, 0, :] = jnp.broadcast_to(total[h:h + 1], (per_head, HEAD_DIM))


def rotated(size):
    return [(size * 5 // 8 + i) % size for i in range(size)]


def send_group(stores, running_ref, out_hbm, sems, first):
    size = max(1, out_hbm.shape[0] // 8)
    part = pl.ds(first, size)
    stores.append(
        pltpu.make_async_copy(running_ref.at[part], out_hbm.at[part], sems.at[first // size])
    )
    stores[-1].start()


def prefix(members_ref, out_hbm, decays_ref, out_ref, sems):
    devices, rows = out_ref.shape[:2]
    order = rotated(devices)
    size = max(1, devices // 8)
    stores = []
    decays_ref[...] = jnp.exp(members_ref[:, rows, 0, :])
    running = jnp.zeros((rows, HEAD_DIM), F32)
    for b in range(devices):
        i = order.index(b)
        out_ref[i] = running
        if (b + 1) % size == 0:
            send_group(stores, out_ref, out_hbm, sems, i // size * size)
        if b < devices - 1:
            running = decays_ref[i:i + 1] * running + members_ref[i, :rows, 0, :]
    for store in stores:
        store.wait()


def suffix(members_ref, decays_ref, out_hbm, after_ref, out_ref, sems):
    after_ref[...] = decays_ref[:1]
    devices, rows = out_ref.shape[:2]
    order = rotated(devices)
    size = max(1, devices // 8)
    stores = []
    running = jnp.zeros((rows, HEAD_DIM), F32)
    for b in reversed(range(devices)):
        i = order.index(b)
        out_ref[i] = running
        if b % size == 0:
            send_group(stores, out_ref, out_hbm, sems, i // size * size)
        if b > 0:
            running = decays_ref[i:i + 1] * running + members_ref[i]
    for store in stores:
        store.wait()


def local_attention(
    queries_ref, keys_ref, values_ref, cum_ref, gain_ref, local_ref, weighted_ref, gain_out_ref
):
    gain_out_ref[...] = gain_ref[...]
    heads = local_ref.shape[1] // HEAD_DIM
    cumulative = cum_ref[...]
    columns = cumulative.T
    growth = jnp.exp(cumulative)
    for h in range(heads):
        cols = head_cols(h)
        weighted = queries_ref[:, cols].T.astype(F32) * growth[h:h + 1]
        weighted_ref[h] = weighted.astype(BF16)
        for start in range(0, BLK, HALF):
            width = start + HALF
            scores = dot(queries_ref[start:width, cols], keys_ref[:width, cols], (1, 1))
            mixing = (scores * decay_tile(cumulative, columns, h, start)).astype(BF16)
            local_ref[start:width, cols] = dot(mixing, values_ref[:width, cols], (1, 0))


def attend(queries_ref, upstream_ref, gain_ref, cum_ref, local_ref, state_ref, att_ref, sums_ref):
    heads = state_ref.shape[0]
    columns = jnp.exp(cum_ref[...]).T
    square = jnp.zeros((BLK, HEAD_DIM), F32)
    cross = jnp.zeros((BLK, HEAD_DIM), F32)
    for h in range(heads):
        cols = head_cols(h)
        high, low = split(state_ref[h])
        carried = dot(twice(queries_ref[:, cols]), jnp.concatenate([high, low], axis=0), (1, 0))
        attended = local_ref[:, cols] + columns[:, h:h + 1] * carried
        att_ref[:, cols] = attended
        scaled = gain_ref[:, cols] * upstream_ref[:, cols].astype(F32)
        square = square + attended * attended
        cross = cross + scaled * attended
    same = eye()
    rows = []
    for summed in (square, cross):
        for j in range(BLK // TILE):
            column = jnp.sum(summed[j * TILE:(j + 1) * TILE], axis=1, keepdims=True)
            rows.append(jnp.sum(jnp.where(same, column, 0.0), axis=0, keepdims=True))
    sums = jnp.concatenate(rows, axis=0)
    for d in range(sums_ref.shape[0]):
        sums_ref[d] = sums


def grad_states(width, sums_ref, att_ref, upstream_ref, gain_ref, weighted_ref, grad_ref, out_ref):
    devices = out_ref.shape[0]
    rows = piece_rows(devices)
    per_head = HEAD_DIM // rows
    heads = devices // per_head
    sums = jnp.sum(sums_ref[...], axis=0)
    tiles = BLK // TILE
    inverse = lax.rsqrt(sums[:tiles] / width + EPSILON)
    pull = inverse * inverse * inverse * sums[tiles:] / width
    scales = jnp.concatenate([inverse, pull], axis=0).T
    for h in range(heads):
        cols = head_cols(h)
        grads = []
        for j in range(tiles):
            part = slice(j * TILE, (j + 1) * TILE)
            scaled = gain_ref[:, cols] * upstream_ref[part, cols].astype(F32)
            grad = scales[:, j:j + 1] * scaled - att_ref[part, cols] * scales[:, tiles + j:tiles + j + 1]
            grads.append(grad.astype(BF16))
            grad_ref[part, cols] = grads[-1]
        state = dot(weighted_ref[h], jnp.concatenate(grads, axis=0), (1, 0))
        out_ref[h * per_head:(h + 1) * per_head] = state.reshape(per_head, rows, HEAD_DIM)


def mix(
    queries_ref, keys_ref, grad_ref, cum_ref, state_ref, after_ref,
    mixing_ref, carried_ref, copy_ref,
):
    del after_ref
    copy_ref[...] = grad_ref[...]
    cumulative = cum_ref[...]
    columns = cumulative.T
    for h in range(mixing_ref.shape[0]):
        cols = head_cols(h)
        for start in range(0, BLK, HALF):
            stop = start + HALF
            scores = dot(queries_ref[start:stop, cols], keys_ref[:stop, cols], (1, 1))
            decays = decay_tile(cumulative, columns, h, start)
            mixing_ref[h, start:stop, :stop] = (scores * decays).astype(BF16)
        high, low = split(state_ref[h])
        carried = dot(twice(grad_ref[:, cols]), jnp.concatenate([high, low], axis=1), (1, 1))
        carried_ref[:, cols] = jnp.exp(columns[:, h:h + 1]) * carried


def local_grads(
    queries_ref, keys_ref, values_ref, grad_ref, cum_ref, mixing_ref, carried_ref,
    grad_queries_ref, grad_keys_ref, grad_values_ref,
):
    heads = mixing_ref.shape[0]
    cumulative = cum_ref[...]
    columns = cumulative.T
    for h in range(heads):
        cols = head_cols(h)
        key_sums, value_sums = [], []
        for start in range(0, BLK, HALF):
            stop = start + HALF
            grad = grad_ref[start:stop, cols]
            decays = decay_tile(cumulative, columns, h, start)
            grad_mixing = (dot(grad, values_ref[:stop, cols], (1, 1)) * decays).astype(BF16)
            grad_query = carried_ref[start:stop, cols] + dot(grad_mixing, keys_ref[:stop, cols], (1, 0))
            grad_queries_ref[start:stop, cols] = grad_query.astype(BF16)
            key_sums.append(dot(queries_ref[start:stop, cols], grad_mixing, (0, 0)))
            value_sums.append(dot(grad, mixing_ref[h, start:stop, :stop], (0, 0)))
        grad_keys_ref[:, cols] = add_halves(*key_sums).T.astype(BF16)
        grad_values_ref[:, cols] = add_halves(*value_sums).T.astype(BF16)


def add_carried(
    keys_ref, values_ref, cum_ref, state_ref, local_keys_ref, local_values_ref,
    grad_keys_hbm, grad_values_hbm, grad_keys_ref, grad_values_ref, sems,
):
    heads = state_ref.shape[0]
    columns = cum_ref[...].T
    stores = []
    for h in range(heads):
        cols = head_cols(h)
        high, low = split(state_ref[h])
        ending = columns[:, heads + h:heads + h + 1]
        grad_key = dot(twice(values_ref[:, cols]), jnp.concatenate([high, low], axis=1), (1, 1))
        grad_value = dot(twice(keys_ref[:, cols]), jnp.concatenate([high, low], axis=0), (1, 0))
        grad_keys_ref[:, cols] = (local_keys_ref[:, cols].astype(F32) + ending * grad_key).astype(BF16)
        grad_values_ref[:, cols] = (local_values_ref[:, cols].astype(F32) + ending * grad_value).astype(BF16)
        for i, (source, target) in enumerate(
            ((grad_keys_ref, grad_keys_hbm), (grad_values_ref, grad_values_hbm))
        ):
            stores.append(
                pltpu.make_async_copy(source.at[:, cols], target.at[:, cols], sems.at[i, h])
            )
            stores[-1].start()
    for store in stores:
        store.wait()


def call(kernel, name, out_shape, *args, flops=0, **options):
    outs = jax.tree.leaves(out_shape)
    size = sum(math.prod(a.shape) * a.dtype.itemsize for a in (*args, *outs))
    return pl.pallas_call(
        kernel,
        out_shape=out_shape,
        name=name,
        compiler_params=pltpu.CompilerParams(vmem_limit_bytes=VMEM_LIMIT),
        cost_estimate=pl.CostEstimate(flops=flops, bytes_accessed=size, transcendentals=0),
        **options,
    )(*args)


def on_device(queries, keys, values, log_decay, gain, upstream):
    tokens, columns = queries.shape
    heads = log_decay.shape[1]
    slabs = lax.axis_size("ctx")
    groups = lax.axis_size("head")
    rows = piece_rows(slabs)
    full_width = columns * groups
    gain = gain[None]
    f32 = functools.partial(jax.ShapeDtypeStruct, dtype=F32)
    bf16 = functools.partial(jax.ShapeDtypeStruct, dtype=BF16)
    square = tokens * tokens * HEAD_DIM * heads * 2
    in_vmem = pl.BlockSpec(memory_space=pltpu.VMEM)
    in_hbm = pl.BlockSpec(memory_space=pltpu.HBM)
    wide = (tokens, columns)

    def exchange(x, axis):
        order = rotated(lax.axis_size(axis))
        return lax.all_to_all(x, axis, 0, 0, tiled=True, axis_index_groups=[order])

    def stay(x):
        return pltpu.with_memory_space_constraint(x, pltpu.HBM)

    pieces, cumulative = call(
        local_states, "local_states", (f32((slabs, rows + 1, 1, HEAD_DIM)), f32((2 * heads, tokens))),
        stay(log_decay.T), stay(keys), stay(values), flops=square // 4,
        in_specs=[in_hbm] * 3,
        scratch_shapes=[
            pltpu.VMEM((heads, tokens), F32),
            pltpu.VMEM(wide, BF16),
            pltpu.VMEM(wide, BF16),
            pltpu.VMEM((heads, HEAD_DIM, tokens), BF16),
            pltpu.SemaphoreType.DMA((3,)),
        ],
    )
    members = exchange(pieces, "ctx")
    local, weighted, gain = call(
        local_attention, "local_attention",
        (f32(wide), pltpu.HBM((heads, HEAD_DIM, tokens), BF16), f32((1, columns))),
        queries, keys, values, cumulative, gain, flops=2 * square,
    )
    starts, decays = call(
        prefix, "prefix",
        (pltpu.HBM((slabs, rows, HEAD_DIM), F32), f32((slabs, HEAD_DIM))), members,
        out_specs=[in_hbm, in_vmem],
        scratch_shapes=[
            pltpu.VMEM((slabs, rows, HEAD_DIM), F32),
            pltpu.SemaphoreType.DMA((8,)),
        ],
    )
    start_state = exchange(starts, "ctx").reshape(heads, HEAD_DIM, HEAD_DIM)
    attended, sums = call(
        attend, "attend", (f32(wide), f32((groups, 2 * tokens // TILE, TILE))),
        queries, upstream, gain, cumulative, local, start_state, flops=square // 2,
    )
    sums = exchange(sums, "head")
    grad_out, grad_pieces = call(
        functools.partial(grad_states, full_width), "grad_states",
        (bf16(wide), f32((slabs, rows, HEAD_DIM))),
        sums, attended, upstream, gain, weighted, flops=square // 4,
    )
    grad_members = exchange(grad_pieces, "ctx")
    ends, after = call(
        suffix, "suffix",
        (pltpu.HBM((slabs, rows, HEAD_DIM), F32), f32((1, HEAD_DIM))), grad_members, decays,
        out_specs=[in_hbm, in_vmem],
        scratch_shapes=[
            pltpu.VMEM((slabs, rows, HEAD_DIM), F32),
            pltpu.SemaphoreType.DMA((8,)),
        ],
    )
    mixing, carried, grad_out = call(
        mix, "mix", (bf16((heads, tokens, tokens)), f32(wide), bf16(wide)),
        queries, keys, grad_out, cumulative, start_state, after, flops=2 * square,
    )
    grad_queries, local_keys, local_values = call(
        local_grads, "local_grads", (bf16(wide), bf16(wide), bf16(wide)),
        queries, keys, values, grad_out, cumulative, mixing, carried, flops=4 * square,
    )
    end_state = exchange(ends, "ctx").reshape(heads, HEAD_DIM, HEAD_DIM)
    grad_keys, grad_values = call(
        add_carried, "add_carried", (bf16(wide), bf16(wide)),
        keys, values, cumulative, end_state, local_keys, local_values, flops=square,
        out_specs=[in_hbm] * 2,
        scratch_shapes=[
            pltpu.VMEM(wide, BF16),
            pltpu.VMEM(wide, BF16),
            pltpu.SemaphoreType.DMA((2, heads)),
        ],
    )
    return grad_queries, grad_keys, grad_values


def solution(mesh):
    placed = (
        P("ctx", "head"),
        P("ctx", "head"),
        P("ctx", "head"),
        P("ctx", "head"),
        P("head"),
        P("ctx", "head"),
    )
    return jax.shard_map(
        on_device,
        mesh=mesh,
        in_specs=placed,
        out_specs=(P("ctx", "head"), P("ctx", "head"), P("ctx", "head")),
        check_vma=False,
    )
```
